32 devices in a mesh: parts: 2 (over y), tok: 8 (over z, x), hid: 2 (over core).
Axes of the slice: x: 2, y: 2, z: 4, core: 2. Of those that a mesh axis runs over, the one named last changes fastest.
Arguments:
- inputs: bfloat16 [2048, 3072], P(('parts', 'tok')), parts along dimension 0
- hidden_grads: bfloat16 [2048, 8192], P(('parts', 'tok')), parts along dimension 0
- routes: int32 [2048, 2], P(('parts', 'tok')), parts along dimension 0, may hold values from 0 to 7, as said below
Outputs:
- input_tiles: float32 [32, 768, 768], P(('parts', 'tok', 'hid')), parts along dimension 0
- grad_tiles: float32 [32, 2048, 2048], P(('parts', 'tok', 'hid')), parts along dimension 0
The draws below stay inside these ranges and needn't reach their ends.
There are 2 independent parts, one for each index of `parts`. The reference program is written for one: setup_inputs(seed, part) draws one part's arguments, and reference() takes and returns one part's arrays. A program takes and returns all parts, laid end to end along the dimension named above; each array names one. Nothing has to cross between parts.
Inputs may be any that keep to these rules, and one draw needn't show every extreme that they name: `routes`: each row names two different experts. Of the 128 rows of one device at most 40 name expert 0, and on some device exactly 40 do.
All inputs are finite; a program needn't handle non-finite values.
Results may differ from the reference program's by a relative error of at most 0.0003.
Values may be sent and summed in bfloat16 or wider, within the bound.
No kernel may reach another device: no remote copies, remote signals or barrier semaphores. Data moves between devices by JAX's collectives and lax.ppermute only.
A program may use at most 128 MiB of HBM per device.

```python
import math
import jax
import jax.numpy as jnp
import numpy as np
from jax import lax

DW = 3072
FW = 8192
EXPERTS = 8
TOP = 2
TOK_DEV = 128
CAP = 40
TOKENS = 1024
SIDE = 4
N_TOK = 8


def scaled_draw(seed_key, noise_part, common_weight):
    row_count, feature_count = noise_part.shape
    key_row, key_col, key_coef, key_vector = jax.random.split(seed_key, 4)
    row_scale = jnp.exp(jax.random.uniform(key_row, (row_count, 1), jnp.float32, math.log(0.3), math.log(3.0)))
    col_scale = jnp.exp(jax.random.uniform(key_col, (1, feature_count), jnp.float32, math.log(0.3), math.log(3.0)))
    coefficient = jnp.clip(jax.random.normal(key_coef, (row_count, 1), jnp.float32), -3.0, 3.0)
    direction = jnp.clip(jax.random.normal(key_vector, (1, feature_count), jnp.float32), -3.0, 3.0)
    return row_scale * col_scale * (noise_part + common_weight * coefficient * direction)


def draw_inputs(key, part):
    key = jax.random.fold_in(key, 3)
    first_key, second_key = jax.random.split(key)
    noise_part = jnp.clip(jax.random.normal(first_key, (TOKENS, DW), jnp.float32), -5.0, 5.0)
    return scaled_draw(second_key, noise_part, 0.5).astype(jnp.bfloat16)


def draw_hidden_grads(key, part):
    key = jax.random.fold_in(key, 5)
    first_key, second_key = jax.random.split(key)
    noise_part = jnp.clip(jax.random.normal(first_key, (TOKENS, FW), jnp.float32), -5.0, 5.0)
    return scaled_draw(second_key, noise_part, 0.5).astype(jnp.bfloat16)


def draw_routes(key, part):
    key = jax.random.fold_in(key, 7)
    key_noise, key_busy, key_rank, key_first, key_offset = jax.random.split(key, 5)
    device_count = TOKENS // TOK_DEV
    device_ids = jnp.arange(device_count, dtype=jnp.int32)
    lowest = CAP // 3
    rising = lowest + (CAP - lowest) * device_ids // max(device_count - 1, 1)
    counts = jnp.clip(rising + jax.random.randint(key_noise, (device_count,), -2, 3), 1, CAP)
    busiest = jax.random.randint(key_busy, (), device_count // 2, device_count)
    counts = jnp.where(device_ids == busiest, CAP, counts)
    ranking = jax.vmap(lambda one_key: jax.random.permutation(one_key, TOK_DEV))(jax.random.split(key_rank, device_count))
    selected = ranking < counts[:, None]
    first_expert = jax.random.randint(key_first, (device_count, TOK_DEV), 1, EXPERTS)
    offsets = jax.random.randint(key_offset, (device_count, TOK_DEV), 1, EXPERTS - 1)
    second_expert = 1 + (first_expert - 1 + offsets) % (EXPERTS - 1)
    leading = jnp.where(selected, 0, first_expert)
    both = jnp.stack([leading, second_expert], axis=-1)
    return both.reshape(TOKENS, TOP).astype(jnp.int32)


def setup_inputs(seed: int = 0, part: int = 0) -> dict:
    streams_of = jax.random.split(jax.random.key(seed), 4)
    own_keys = jax.random.split(jax.random.fold_in(streams_of[3], part), 4)
    inputs = draw_inputs(jax.random.fold_in(jax.random.fold_in(streams_of[3], part), 71), part)
    hidden_grads = draw_hidden_grads(jax.random.fold_in(jax.random.fold_in(streams_of[3], part), 71), part)
    routes = draw_routes(jax.random.fold_in(jax.random.fold_in(streams_of[3], part), 71), part)
    return dict(inputs=inputs, hidden_grads=hidden_grads, routes=routes)


def block_table(side):
    first_list = []
    second_list = []
    for owner_chip in range(side * side // 2):
        stripe = owner_chip // side
        column = owner_chip % side
        if column == side - 1:
            first_list.append(stripe)
            second_list.append(side - 1 - stripe)
        elif column < side - 1 - stripe:
            first_list.append(stripe)
            second_list.append(stripe + 1 + column)
        else:
            first_list.append(side - 1 - stripe)
            second_list.append(column + 1)
    return np.array(first_list, np.int32), np.array(second_list, np.int32)


def tile_indices(side):
    first_ids, second_ids = block_table(side)
    row_list = []
    col_list = []
    for owner_chip in range(side * side // 2):
        first_block = int(first_ids[owner_chip])
        second_block = int(second_ids[owner_chip])
        if owner_chip % side == side - 1:
            row_list += [first_block, second_block]
            col_list += [first_block, second_block]
        else:
            row_list += [first_block, second_block]
            col_list += [second_block, first_block]
    return np.array(row_list, np.int32), np.array(col_list, np.int32)


def compacted(values, chosen):
    feature_count = values.shape[1]
    blocks = values.reshape(N_TOK, TOK_DEV, feature_count)
    flags = chosen.reshape(N_TOK, TOK_DEV)
    ordering = jnp.argsort(1 - flags, axis=1, stable=True)[:, :CAP]
    kept = jnp.take_along_axis(flags, ordering, axis=1)
    picked = jax.vmap(lambda block, order_row: block[order_row])(blocks, ordering)
    picked = picked.reshape(N_TOK * CAP, feature_count).astype(jnp.float32)
    return picked * kept.reshape(N_TOK * CAP, 1).astype(jnp.float32)


def factor_tiles(values, chosen, count):
    feature_count = values.shape[1]
    picked = compacted(values, chosen)
    factor = jnp.dot(picked.T, picked, precision=lax.Precision.HIGHEST) / count
    size = feature_count // SIDE
    grid = factor.reshape(SIDE, size, SIDE, size)
    row_ids, col_ids = tile_indices(SIDE)
    return grid[row_ids, :, col_ids, :]


def reference(inputs, hidden_grads, routes):
    chosen = jnp.any(routes == 0, axis=1).astype(jnp.int32)
    count = jnp.sum(chosen).astype(jnp.float32)
    return factor_tiles(inputs, chosen, count), factor_tiles(hidden_grads, chosen, count)
```

```python
import functools
import math

import jax
import jax.numpy as jnp
import numpy as np
from jax import lax
from jax.experimental import pallas as pl
from jax.experimental.pallas import tpu as pltpu
from jax.sharding import PartitionSpec as P

VMEM_LIMIT = 56 * 1024 * 1024
SLOT_ROWS = 48


def block_table(side):
    first_list = []
    second_list = []
    for owner_chip in range(side * side // 2):
        stripe = owner_chip // side
        column = owner_chip % side
        if column == side - 1:
            first_list.append(stripe)
            second_list.append(side - 1 - stripe)
        elif column < side - 1 - stripe:
            first_list.append(stripe)
            second_list.append(stripe + 1 + column)
        else:
            first_list.append(side - 1 - stripe)
            second_list.append(column + 1)
    return (np.array(first_list, np.int32), np.array(second_list, np.int32))


def compact(values, chosen, capacity):
    ranking = jnp.cumsum(chosen) - 1
    slot_ids = jnp.arange(capacity, dtype=jnp.int32)
    picker = ((ranking[None, :] == slot_ids[:, None]) & (chosen[None, :] == 1)).astype(jnp.bfloat16)
    return jnp.dot(picker, values, preferred_element_type=jnp.float32).astype(jnp.bfloat16)


def outgoing(packed, side, first_ids, second_ids):
    slot_count, feature_count = packed.shape
    blocks = packed.reshape(slot_count, side, feature_count // side)
    return jnp.concatenate([blocks[:, first_ids], blocks[:, second_ids]], axis=2)


def product(flat_data, left_start, right_start, width):
    left = lax.dynamic_slice_in_dim(flat_data, left_start, width, 1)
    right = lax.dynamic_slice_in_dim(flat_data, right_start, width, 1)
    return lax.dot_general(
        left, right, (((0,), (0,)), ((), ())), preferred_element_type=jnp.float32
    )


def shards_any(inputs, hidden_grads, routes):
    chosen = jnp.any(routes == 0, axis=1).astype(jnp.int32)
    core_index = lax.axis_index("hid")
    chip_index = lax.axis_index("tok")
    device_count = lax.axis_size("tok")
    side = math.isqrt(2 * device_count)
    first_ids, second_ids = block_table(side)
    diagonal = chip_index % side == side - 1
    capacity = chosen.shape[0] * 5 // 16
    packed_inputs = compact(inputs, chosen, capacity)
    packed_grads = compact(hidden_grads, chosen, capacity)
    send_inputs = outgoing(packed_inputs, side, first_ids, second_ids)
    send_grads = outgoing(packed_grads, side, first_ids, second_ids)
    local_count = jnp.sum(chosen)
    got_inputs = lax.all_to_all(send_inputs, "tok", split_axis=1, concat_axis=1, tiled=True)
    total = lax.psum(local_count.astype(jnp.float32), "tok")
    got_grads = lax.all_to_all(send_grads, "tok", split_axis=1, concat_axis=1, tiled=True)
    flat_inputs = got_inputs.reshape(-1, got_inputs.shape[2])
    flat_grads = got_grads.reshape(-1, got_grads.shape[2])
    input_width = flat_inputs.shape[1] // 2
    grad_width = flat_grads.shape[1] // 2
    right_pick = jnp.where(diagonal, core_index, 1 - core_index)
    input_sum = product(
        flat_inputs, core_index * input_width, right_pick * input_width, input_width
    )
    grad_sum = product(flat_grads, core_index * grad_width, right_pick * grad_width, grad_width)
    return ((input_sum / total)[None], (grad_sum / total)[None])


N_X = 2
N_Z = 4


def slot_table():
    first_ids, second_ids = block_table(4)
    slots = np.zeros((N_Z, N_X, 3), np.int32)
    for z in range(N_Z):
        zero = {int(first_ids[z * N_X]), int(second_ids[z * N_X])}
        one = {int(first_ids[z * N_X + 1]), int(second_ids[z * N_X + 1])}
        common = max(zero & one)
        (a,) = zero - {common}
        (b,) = one - {common}
        slots[z, 0] = (a, common, b)
        slots[z, 1] = (b, common, a)
    return slots


def pack_kernel(mark, table_ref, routes_ref, values_ref, own_ref, x_ref, *rest):
    z_refs, half_ref = rest[:-1], rest[-1]
    capacity, half = x_ref.shape[1:]
    width = 2 * half
    chosen = (routes_ref[0:1, :] == 0) | (routes_ref[1:2, :] == 0)
    tokens = chosen.shape[1]
    flags = jnp.where(chosen, 1.0, 0.0)
    before = (
        lax.broadcasted_iota(jnp.int32, (tokens, tokens), 0)
        <= lax.broadcasted_iota(jnp.int32, (tokens, tokens), 1)
    )
    rank = jnp.dot(
        flags.astype(jnp.bfloat16),
        jnp.where(before, 1.0, 0.0).astype(jnp.bfloat16),
        preferred_element_type=jnp.float32,
    )
    count = jnp.sum(flags)
    slot = lax.broadcasted_iota(jnp.int32, (capacity, tokens), 0).astype(jnp.float32) + 1.0
    picker = jnp.where((rank == slot) & chosen, 1.0, 0.0).astype(jnp.bfloat16)
    core = table_ref[0]
    empty = (
        (lax.broadcasted_iota(jnp.int32, (capacity, 128), 0).astype(jnp.float32) >= count)
        & (lax.broadcasted_iota(jnp.int32, (capacity, 128), 1) == 0)
    )

    def pick(block, part):
        start = pl.multiple_of(block * width + part * half, 128)
        return jnp.dot(
            picker, values_ref[:, pl.ds(start, half)], preferred_element_type=jnp.float32
        )

    def put(ref, row, column, block, part):
        got = pick(block, part)
        if mark:
            head = jnp.where(empty & (part == 0), jnp.inf, got[:, :128])
            ref[row, :, column : column + 128] = head.astype(jnp.bfloat16)
            ref[row, :, column + 128 : column + half] = got[:, 128:].astype(jnp.bfloat16)
        else:
            ref[row, :, column : column + half] = got.astype(jnp.bfloat16)

    for block in range(4):
        put(half_ref, block, 0, block, core)
    for i, ref in enumerate(z_refs):
        for row in range(3):
            ref[row] = half_ref[table_ref[4 + 3 * i + row]]
    for row in range(2):
        x_ref[row] = half_ref[table_ref[2 + row]]
    for row in range(2):
        for part in range(2):
            put(own_ref, row, part * half, table_ref[1 + row], part)


def pack(mark, table, routes_t, values, capacity):
    half = values.shape[1] // 8
    shapes = [(2, capacity, 2 * half), (2, capacity, half)] + [(3, capacity, half)] * 3
    vmem = pl.BlockSpec(memory_space=pltpu.VMEM)
    return pl.pallas_call(
        functools.partial(pack_kernel, mark),
        out_shape=[jax.ShapeDtypeStruct(s, jnp.bfloat16) for s in shapes],
        in_specs=[pl.BlockSpec(memory_space=pltpu.SMEM), vmem, vmem],
        out_specs=[vmem] * len(shapes),
        scratch_shapes=[pltpu.VMEM((4, capacity, half), jnp.bfloat16)],
        compiler_params=pltpu.CompilerParams(vmem_limit_bytes=VMEM_LIMIT),
        cost_estimate=pl.CostEstimate(
            flops=2 * capacity * values.size, bytes_accessed=2 * values.size, transcendentals=0
        ),
    )(table, routes_t, values)


def tile_kernel(marked, table_ref, *refs):
    refs = list(refs)
    count_in = None if marked else refs.pop(0)
    own_ref = refs.pop(0)
    z_refs = [refs.pop(0) for _ in range(3)]
    hz_refs = [refs.pop(0) for _ in range(3)]
    x_refs = [refs.pop(0) for _ in range(4)]
    hx_refs = [refs.pop(0) for _ in range(4)]
    out_ref = refs.pop(0)
    count_out = refs.pop(0) if marked else None
    data_ref, scale_ref = refs
    capacity, half = x_refs[0].shape[1:]
    step = pl.program_id(0)
    rows_out = out_ref.shape[1]
    core = table_ref[0]
    left = table_ref[1]
    right = table_ref[2]

    @pl.when(step == 0)
    def _():
        slots = data_ref.shape[1] // SLOT_ROWS
        for block in range(2):
            for slot in range(slots):
                data_ref[block, slot * SLOT_ROWS + 32 : (slot + 1) * SLOT_ROWS, :] = jnp.zeros(
                    (SLOT_ROWS - 32, 2 * half), jnp.bfloat16
                )
        mine = pl.multiple_of(core * half, 128)
        other = pl.multiple_of((1 - core) * half, 128)
        for block in range(2):
            data_ref[block, 0:capacity, :] = own_ref[block]
            for i in range(3):
                rows = pl.ds((1 + i) * SLOT_ROWS, capacity)
                data_ref[block, rows, pl.ds(mine, half)] = z_refs[i][block]
                data_ref[block, rows, pl.ds(other, half)] = hz_refs[i][block]
            for i in range(4):
                rows = pl.ds((4 + i) * SLOT_ROWS, capacity)
                data_ref[block, rows, pl.ds(mine, half)] = x_refs[i][1 - block]
                data_ref[block, rows, pl.ds(other, half)] = hx_refs[i][1 - block]
        if marked:
            for block in range(2):
                head = data_ref[block, :, 0:128].astype(jnp.float32)
                gone = head == jnp.inf
                if block == 0:
                    count = capacity * slots - jnp.sum(jnp.where(gone, 1.0, 0.0))
                    scale_ref[0] = 1.0 / count
                    count_out[0] = 1.0 / count
                data_ref[block, :, 0:128] = jnp.where(gone, 0.0, head).astype(jnp.bfloat16)
        else:
            scale_ref[0] = count_in[0]

    start = pl.multiple_of(step * rows_out, rows_out)
    product_ = lax.dot_general(
        data_ref[left, :, pl.ds(start, rows_out)],
        data_ref[right],
        (((0,), (0,)), ((), ())),
        preferred_element_type=jnp.float32,
    )
    out_ref[0] = product_ * scale_ref[0]


def tile(table, scale, own, z_got, hz_got, x_got, hx_got, rows_out):
    marked = scale is None
    width = own.shape[2]
    operands = [table] + ([] if marked else [scale]) + [own, *z_got, *hz_got, *x_got, *hx_got]
    smem = pl.BlockSpec(memory_space=pltpu.SMEM)
    vmem = pl.BlockSpec(memory_space=pltpu.VMEM)
    n_smem = 1 if marked else 2
    out_shape = [jax.ShapeDtypeStruct((1, width, width), jnp.float32)]
    out_specs = [pl.BlockSpec((1, rows_out, width), lambda i: (0, i, 0))]
    if marked:
        out_shape.append(jax.ShapeDtypeStruct((1,), jnp.float32))
        out_specs.append(smem)
    slots = 8
    return pl.pallas_call(
        functools.partial(tile_kernel, marked),
        grid=(width // rows_out,),
        out_shape=out_shape,
        in_specs=[smem] * n_smem + [vmem] * (len(operands) - n_smem),
        out_specs=out_specs,
        scratch_shapes=[
            pltpu.VMEM((2, slots * SLOT_ROWS, width), jnp.bfloat16),
            pltpu.SMEM((1,), jnp.float32),
        ],
        compiler_params=pltpu.CompilerParams(vmem_limit_bytes=VMEM_LIMIT),
        cost_estimate=pl.CostEstimate(
            flops=2 * slots * SLOT_ROWS * width * width,
            bytes_accessed=4 * width * width,
            transcendentals=0,
        ),
    )(*operands)


def z_pairs(distance):
    return [
        (z * N_X + x, ((z + distance) % N_Z) * N_X + x) for z in range(N_Z) for x in range(N_X)
    ]


X_PAIRS = [(chip, chip ^ 1) for chip in range(N_Z * N_X)]
CORE_PAIRS = [(0, 1), (1, 0)]


def spread(own, x_send, z_sends):
    z_got = [lax.ppermute(send, "tok", z_pairs(d)) for d, send in zip((1, 3, 2), z_sends)]
    x_got = [lax.ppermute(x_send, "tok", X_PAIRS)]
    x_got += [lax.ppermute(got[1:], "tok", X_PAIRS) for got in z_got]
    hz_got = [lax.ppermute(got[:2], "hid", CORE_PAIRS) for got in z_got]
    hx_got = [lax.ppermute(got, "hid", CORE_PAIRS) for got in x_got]
    return own, z_got, hz_got, x_got, hx_got


def shards_eight(inputs, hidden_grads, routes):
    core = lax.axis_index("hid").astype(jnp.int32)
    chip = lax.axis_index("tok").astype(jnp.int32)
    plane, column = chip // N_X, chip % N_X
    capacity = routes.shape[0] * 5 // 16
    slots = jnp.asarray(slot_table())
    entries = [core[None], slots[plane, column]]
    entries += [slots[(plane + d) % N_Z, column] for d in (1, 3, 2)]
    pack_table = jnp.concatenate(entries)
    first_ids, second_ids = block_table(4)
    keep = slot_table()[np.arange(8) // N_X, np.arange(8) % N_X, 0]
    first_is_common = jnp.asarray((keep != first_ids).astype(np.int32))[chip]
    diagonal = (chip % 4 == 3).astype(jnp.int32)
    left = jnp.where(core == 0, first_is_common, 1 - first_is_common)
    right = jnp.where(diagonal == 1, left, 1 - left)
    tile_table = jnp.stack([core, left, right])
    routes_t = routes.T
    own, x_send, *z_sends = pack(True, pack_table, routes_t, hidden_grads, capacity)
    own_i, x_send_i, *z_sends_i = pack(False, pack_table, routes_t, inputs, capacity)
    grad_parts = spread(own, x_send, z_sends)
    input_parts = spread(own_i, x_send_i, z_sends_i)
    grad_tile, scale = tile(tile_table, None, *grad_parts, 256)
    (input_tile,) = tile(tile_table, scale, *input_parts, 256)
    return input_tile, grad_tile


def solution(mesh):
    placed = (P(("parts", "tok"), None), P(("parts", "tok"), None), P(("parts", "tok"), None))
    return jax.shard_map(
        shards_eight if mesh.shape["tok"] == N_X * N_Z else shards_any,
        mesh=mesh,
        in_specs=placed,
        out_specs=(P(("parts", "tok", "hid"), None, None), P(("parts", "tok", "hid"), None, None)),
        check_vma=False,
    )
```

```python
import functools
import math

import jax
import jax.numpy as jnp
import numpy as np
from jax import lax
from jax.experimental import pallas as pl
from jax.experimental.pallas import tpu as pltpu
from jax.sharding import PartitionSpec as P

SLOT_ROWS = 48


def block_table(side):
    first_list = []
    second_list = []
    for owner_chip in range(side * side // 2):
        stripe = owner_chip // side
        column = owner_chip % side
        if column == side - 1:
            first_list.append(stripe)
            second_list.append(side - 1 - stripe)
        elif column < side - 1 - stripe:
            first_list.append(stripe)
            second_list.append(stripe + 1 + column)
        else:
            first_list.append(side - 1 - stripe)
            second_list.append(column + 1)
    return (np.array(first_list, np.int32), np.array(second_list, np.int32))


def compact(values, chosen, capacity):
    ranking = jnp.cumsum(chosen) - 1
    slot_ids = jnp.arange(capacity, dtype=jnp.int32)
    picker = ((ranking[None, :] == slot_ids[:, None]) & (chosen[None, :] == 1)).astype(jnp.bfloat16)
    return jnp.dot(picker, values, preferred_element_type=jnp.float32).astype(jnp.bfloat16)


def outgoing(packed, side, first_ids, second_ids):
    slot_count, feature_count = packed.shape
    blocks = packed.reshape(slot_count, side, feature_count // side)
    return jnp.concatenate([blocks[:, first_ids], blocks[:, second_ids]], axis=2)


def product(flat_data, left_start, right_start, width):
    left = lax.dynamic_slice_in_dim(flat_data, left_start, width, 1)
    right = lax.dynamic_slice_in_dim(flat_data, right_start, width, 1)
    return lax.dot_general(
        left, right, (((0,), (0,)), ((), ())), preferred_element_type=jnp.float32
    )


def shards_any(inputs, hidden_grads, routes):
    chosen = jnp.any(routes == 0, axis=1).astype(jnp.int32)
    core_index = lax.axis_index("hid")
    chip_index = lax.axis_index("tok")
    device_count = lax.axis_size("tok")
    side = math.isqrt(2 * device_count)
    first_ids, second_ids = block_table(side)
    diagonal = chip_index % side == side - 1
    capacity = chosen.shape[0] * 5 // 16
    packed_inputs = compact(inputs, chosen, capacity)
    packed_grads = compact(hidden_grads, chosen, capacity)
    send_inputs = outgoing(packed_inputs, side, first_ids, second_ids)
    send_grads = outgoing(packed_grads, side, first_ids, second_ids)
    local_count = jnp.sum(chosen)
    got_inputs = lax.all_to_all(send_inputs, "tok", split_axis=1, concat_axis=1, tiled=True)
    total = lax.psum(local_count.astype(jnp.float32), "tok")
    got_grads = lax.all_to_all(send_grads, "tok", split_axis=1, concat_axis=1, tiled=True)
    flat_inputs = got_inputs.reshape(-1, got_inputs.shape[2])
    flat_grads = got_grads.reshape(-1, got_grads.shape[2])
    input_width = flat_inputs.shape[1] // 2
    grad_width = flat_grads.shape[1] // 2
    right_pick = jnp.where(diagonal, core_index, 1 - core_index)
    input_sum = product(
        flat_inputs, core_index * input_width, right_pick * input_width, input_width
    )
    grad_sum = product(flat_grads, core_index * grad_width, right_pick * grad_width, grad_width)
    return ((input_sum / total)[None], (grad_sum / total)[None])


N_X = 2
N_Z = 4


def slot_table():
    first_ids, second_ids = block_table(4)
    slots = np.zeros((N_Z, N_X, 3), np.int32)
    for z in range(N_Z):
        zero = {int(first_ids[z * N_X]), int(second_ids[z * N_X])}
        one = {int(first_ids[z * N_X + 1]), int(second_ids[z * N_X + 1])}
        common = max(zero & one)
        (a,) = zero - {common}
        (b,) = one - {common}
        slots[z, 0] = (a, common, b)
        slots[z, 1] = (b, common, a)
    return slots


def lookup(values, index):
    found = jnp.int32(int(values[0]))
    for i in range(1, len(values)):
        found = jnp.where(index == i, jnp.int32(int(values[i])), found)
    return found


def place():
    chip = lax.axis_index("tok").astype(jnp.int32)
    return lax.div(chip, N_X), lax.rem(chip, N_X), lax.axis_index("hid").astype(jnp.int32)


def pack_kernel(mark, routes_ref, values_ref, p1_ref, p2_ref, x0_ref, own_ref, held, packed, sems):
    plane, column, core = place()
    capacity, half = p2_ref.shape[1:]
    width = 2 * half
    copies = [
        pltpu.make_async_copy(
            values_ref.at[:, block * width : (block + 1) * width], held.at[block], sems.at[block]
        )
        for block in range(4)
    ]
    for copy in copies:
        copy.start()
    chosen = (routes_ref[0:1, :] == 0) | (routes_ref[1:2, :] == 0)
    tokens = chosen.shape[1]
    flags = jnp.where(chosen, 1.0, 0.0)
    before = (
        lax.broadcasted_iota(jnp.int32, (tokens, tokens), 0)
        <= lax.broadcasted_iota(jnp.int32, (tokens, tokens), 1)
    )
    rank = jnp.dot(
        flags.astype(jnp.bfloat16),
        jnp.where(before, 1.0, 0.0).astype(jnp.bfloat16),
        preferred_element_type=jnp.float32,
    )
    slot = lax.broadcasted_iota(jnp.int32, (capacity, tokens), 0).astype(jnp.float32) + 1.0
    picker = jnp.where((rank == slot) & chosen, 1.0, 0.0)
    empty = (jnp.sum(picker, axis=1, keepdims=True) == 0.0) & (
        lax.broadcasted_iota(jnp.int32, (capacity, 128), 1) == 0
    )
    picker = picker.astype(jnp.bfloat16)
    for block in range(4):
        copies[block].wait()
        got = jnp.dot(picker, held[block], preferred_element_type=jnp.float32)
        if mark:
            head = jnp.where(empty, jnp.inf, got[:, :128])
            packed[block, :, :128] = head.astype(jnp.bfloat16)
            packed[block, :, 128:] = got[:, 128:].astype(jnp.bfloat16)
        else:
            packed[block] = got.astype(jnp.bfloat16)

    table = slot_table().reshape(-1, 3)

    def block_at(to_plane, row):
        return lookup(table[:, row], to_plane * N_X + column)

    to_plane = lax.rem(plane + jnp.where(core == 0, 1, 3), N_Z)
    for row in range(3):
        p1_ref[row] = packed[block_at(to_plane, row)]
    start = pl.multiple_of(core * half, 128)
    for row in range(2):
        x0_ref[row] = packed[block_at(plane, row + 1), :, pl.ds(start, half)]
    to_plane = lax.rem(plane + 2, N_Z)
    for row in range(3):
        p2_ref[row] = packed[block_at(to_plane, row), :, pl.ds(start, half)]
    for row in range(2):
        own_ref[row] = packed[block_at(plane, row)]


def pack(mark, routes_t, values, capacity):
    tokens = values.shape[0]
    width = values.shape[1] // 4
    half = width // 2
    shapes = [(3, capacity, width), (3, capacity, half), (2, capacity, half), (2, capacity, width)]
    vmem = pl.BlockSpec(memory_space=pltpu.VMEM)
    return pl.pallas_call(
        functools.partial(pack_kernel, mark),
        out_shape=[jax.ShapeDtypeStruct(s, jnp.bfloat16) for s in shapes],
        in_specs=[vmem, pl.BlockSpec(memory_space=pl.ANY)],
        out_specs=[vmem] * len(shapes),
        scratch_shapes=[
            pltpu.VMEM((4, tokens, width), jnp.bfloat16),
            pltpu.VMEM((4, capacity, width), jnp.bfloat16),
            pltpu.SemaphoreType.DMA((4,)),
        ],
        compiler_params=pltpu.CompilerParams(vmem_limit_bytes=12 * 2**20),
        cost_estimate=pl.CostEstimate(
            flops=2 * capacity * values.size, bytes_accessed=2 * values.size, transcendentals=0
        ),
    )(routes_t, values)


def tile_kernel(marked, *refs):
    refs = list(refs)
    scale_in = None if marked else refs.pop(0)
    own, p1, hp1, p2, hp2, x0, hx0, x1, hx1, x2, hx2 = (refs.pop(0) for _ in range(11))
    out_ref = refs.pop(0)
    scale_out = refs.pop(0) if marked else None
    data, stage, sems = refs
    plane, column, core = place()
    chip = plane * N_X + column
    capacity, half = p2.shape[1:]
    width = 2 * half
    rows_out = width // sems.shape[0]
    slots = data.shape[1] // SLOT_ROWS
    first_ids, _ = block_table(4)
    first_is_common = lookup(
        (slot_table().reshape(-1, 3)[:, 0] != first_ids).astype(np.int32), chip
    )
    left = jnp.where(core == 0, first_is_common, 1 - first_is_common)
    right = jnp.where(lax.rem(chip, 4) == 3, left, 1 - left)

    mine = pl.multiple_of(core * half, 128)
    other = pl.multiple_of((1 - core) * half, 128)
    for block in range(2):
        for slot in range(slots):
            data[block, slot * SLOT_ROWS + 32 : (slot + 1) * SLOT_ROWS, :] = jnp.zeros(
                (SLOT_ROWS - 32, width), jnp.bfloat16
            )
        whole = (own.at[block], p1.at[block], hp1.at[block], x1.at[1 - block], hx1.at[1 - block])
        for slot, ref in enumerate(whole):
            data[block, slot * SLOT_ROWS : slot * SLOT_ROWS + capacity, :] = ref[...]
        halves = (
            (p2.at[block], hp2.at[block]),
            (x0.at[1 - block], hx0.at[1 - block]),
            (x2.at[1 - block], hx2.at[1 - block]),
        )
        for slot, (ref, far_ref) in enumerate(halves, len(whole)):
            rows = pl.ds(slot * SLOT_ROWS, capacity)
            data[block, rows, pl.ds(mine, half)] = ref[...]
            data[block, rows, pl.ds(other, half)] = far_ref[...]
    if marked:
        for block in range(2):
            head = data[block, :, 0:128].astype(jnp.float32)
            gone = head == jnp.inf
            if block == 0:
                scale = 1.0 / (capacity * slots - jnp.sum(jnp.where(gone, 1.0, 0.0)))
                scale_out[0] = scale
            data[block, :, 0:128] = jnp.where(gone, 0.0, head).astype(jnp.bfloat16)
    else:
        scale = scale_in[0]

    copies = []
    for i in range(sems.shape[0]):
        rows = pl.ds(i * rows_out, rows_out)
        stage[rows, :] = scale * lax.dot_general(
            data[left, :, rows],
            data[right],
            (((0,), (0,)), ((), ())),
            preferred_element_type=jnp.float32,
        )
        copies.append(pltpu.make_async_copy(stage.at[rows], out_ref.at[0, rows], sems.at[i]))
        copies[-1].start()
    for copy in copies:
        copy.wait()


def tile(scale, parts, steps, limit):
    marked = scale is None
    width = parts[0].shape[2]
    smem = pl.BlockSpec(memory_space=pltpu.SMEM)
    vmem = pl.BlockSpec(memory_space=pltpu.VMEM)
    out_shape = [jax.ShapeDtypeStruct((1, width, width), jnp.float32)]
    out_specs = [pl.BlockSpec(memory_space=pl.ANY)]
    if marked:
        out_shape.append(jax.ShapeDtypeStruct((1,), jnp.float32))
        out_specs.append(smem)
    slots = 8
    return pl.pallas_call(
        functools.partial(tile_kernel, marked),
        out_shape=out_shape,
        in_specs=([] if marked else [smem]) + [vmem] * len(parts),
        out_specs=out_specs,
        scratch_shapes=[
            pltpu.VMEM((2, slots * SLOT_ROWS, width), jnp.bfloat16),
            pltpu.VMEM((width, width), jnp.float32),
            pltpu.SemaphoreType.DMA((steps,)),
        ],
        compiler_params=pltpu.CompilerParams(vmem_limit_bytes=limit),
        cost_estimate=pl.CostEstimate(
            flops=2 * slots * SLOT_ROWS * width * width,
            bytes_accessed=4 * width * width,
            transcendentals=0,
        ),
    )(*([] if marked else [scale]), *parts)


def moves(step):
    pairs = []
    for z in range(N_Z):
        for x in range(N_X):
            for core in range(2):
                to_z, to_x, to_core = step(z, x, core)
                source = (z * N_X + x) * 2 + core
                pairs.append((source, (to_z % N_Z * N_X + to_x) * 2 + to_core))
    return pairs


ALONG_Z = moves(lambda z, x, core: (z + (1, 3)[core], x, core))
ACROSS_Z = moves(lambda z, x, core: (z + 2, x, core))
ALONG_X = moves(lambda z, x, core: (z, 1 - x, core))
CORES = moves(lambda z, x, core: (z, x, 1 - core))


def send(array, pairs, after=()):
    if after:
        array = lax.optimization_barrier((array, *after))[0]
    return lax.ppermute(array, ("tok", "hid"), pairs)


def shards_eight(inputs, hidden_grads, routes):
    capacity = routes.shape[0] * 5 // 16
    routes_t = routes.T
    p1, p2, x0, own = pack(True, routes_t, hidden_grads, capacity)
    p1 = send(p1, ALONG_Z)
    x0 = send(x0, ALONG_X)
    p1_i, p2_i, x0_i, own_i = pack(False, routes_t, inputs, capacity)
    x0_i = send(x0_i, ALONG_X)
    p2 = send(p2, ACROSS_Z, [x0, x0_i])
    hx0 = send(x0, CORES)
    hx0_i = send(x0_i, CORES)
    x1 = send(p1[1:], ALONG_X)
    hp1 = send(p1[:2], CORES)
    p1_i = send(p1_i, ALONG_Z, [p1])
    hx1 = send(x1, CORES)
    x2 = send(p2[1:], ALONG_X)
    hp2 = send(p2[:2], CORES)
    p2_i = send(p2_i, ACROSS_Z, [p2])
    hx2 = send(x2, CORES)
    x1_i = send(p1_i[1:], ALONG_X, [x2])
    hp1_i = send(p1_i[:2], CORES)
    hx1_i = send(x1_i, CORES)
    x2_i = send(p2_i[1:], ALONG_X)
    hp2_i = send(p2_i[:2], CORES)
    hx2_i = send(x2_i, CORES)
    grad_tile, scale = tile(
        None, (own, p1, hp1, p2, hp2, x0, hx0, x1, hx1, x2, hx2), 8, 28 * 2**20
    )
    (input_tile,) = tile(
        scale,
        (own_i, p1_i, hp1_i, p2_i, hp2_i, x0_i, hx0_i, x1_i, hx1_i, x2_i, hx2_i),
        3,
        12 * 2**20,
    )
    return input_tile, grad_tile


def solution(mesh):
    placed = (P(("parts", "tok"), None), P(("parts", "tok"), None), P(("parts", "tok"), None))
    return jax.shard_map(
        shards_eight if mesh.shape["tok"] == N_X * N_Z else shards_any,
        mesh=mesh,
        in_specs=placed,
        out_specs=(P(("parts", "tok", "hid"), None, None), P(("parts", "tok", "hid"), None, None)),
        check_vma=False,
    )
```

```python
import functools
import math

import jax
import jax.numpy as jnp
import numpy as np
from jax import lax
from jax.experimental import pallas as pl
from jax.experimental.pallas import tpu as pltpu
from jax.sharding import PartitionSpec as P

SLOT_ROWS = 48


def block_table(side):
    first_list = []
    second_list = []
    for owner_chip in range(side * side // 2):
        stripe = owner_chip // side
        column = owner_chip % side
        if column == side - 1:
            first_list.append(stripe)
            second_list.append(side - 1 - stripe)
        elif column < side - 1 - stripe:
            first_list.append(stripe)
            second_list.append(stripe + 1 + column)
        else:
            first_list.append(side - 1 - stripe)
            second_list.append(column + 1)
    return (np.array(first_list, np.int32), np.array(second_list, np.int32))


def compact(values, chosen, capacity):
    ranking = jnp.cumsum(chosen) - 1
    slot_ids = jnp.arange(capacity, dtype=jnp.int32)
    picker = ((ranking[None, :] == slot_ids[:, None]) & (chosen[None, :] == 1)).astype(jnp.bfloat16)
    return jnp.dot(picker, values, preferred_element_type=jnp.float32).astype(jnp.bfloat16)


def outgoing(packed, side, first_ids, second_ids):
    slot_count, feature_count = packed.shape
    blocks = packed.reshape(slot_count, side, feature_count // side)
    return jnp.concatenate([blocks[:, first_ids], blocks[:, second_ids]], axis=2)


def block_product(flat_data, left_start, right_start, width):
    left = lax.dynamic_slice_in_dim(flat_data, left_start, width, 1)
    right = lax.dynamic_slice_in_dim(flat_data, right_start, width, 1)
    return lax.dot_general(
        left, right, (((0,), (0,)), ((), ())), preferred_element_type=jnp.float32
    )


def shards_any(inputs, hidden_grads, routes):
    chosen = jnp.any(routes == 0, axis=1).astype(jnp.int32)
    core_index = lax.axis_index("hid")
    chip_index = lax.axis_index("tok")
    device_count = lax.axis_size("tok")
    side = math.isqrt(2 * device_count)
    first_ids, second_ids = block_table(side)
    diagonal = chip_index % side == side - 1
    capacity = chosen.shape[0] * 5 // 16
    packed_inputs = compact(inputs, chosen, capacity)
    packed_grads = compact(hidden_grads, chosen, capacity)
    send_inputs = outgoing(packed_inputs, side, first_ids, second_ids)
    send_grads = outgoing(packed_grads, side, first_ids, second_ids)
    local_count = jnp.sum(chosen)
    got_inputs = lax.all_to_all(send_inputs, "tok", split_axis=1, concat_axis=1, tiled=True)
    total = lax.psum(local_count.astype(jnp.float32), "tok")
    got_grads = lax.all_to_all(send_grads, "tok", split_axis=1, concat_axis=1, tiled=True)
    flat_inputs = got_inputs.reshape(-1, got_inputs.shape[2])
    flat_grads = got_grads.reshape(-1, got_grads.shape[2])
    input_width = flat_inputs.shape[1] // 2
    grad_width = flat_grads.shape[1] // 2
    right_pick = jnp.where(diagonal, core_index, 1 - core_index)
    input_sum = block_product(
        flat_inputs, core_index * input_width, right_pick * input_width, input_width
    )
    grad_sum = block_product(flat_grads, core_index * grad_width, right_pick * grad_width, grad_width)
    return ((input_sum / total)[None], (grad_sum / total)[None])


N_X = 2
N_Z = 4
SLOTS = N_X * N_Z
SMEM = pl.BlockSpec(memory_space=pltpu.SMEM)
VMEM = pl.BlockSpec(memory_space=pltpu.VMEM)
ANY = pl.BlockSpec(memory_space=pl.ANY)


def slot_table():
    first_ids, second_ids = block_table(4)
    slots = np.zeros((N_Z, N_X, 3), np.int32)
    for z in range(N_Z):
        zero = {int(first_ids[z * N_X]), int(second_ids[z * N_X])}
        one = {int(first_ids[z * N_X + 1]), int(second_ids[z * N_X + 1])}
        common = max(zero & one)
        (a,) = zero - {common}
        (b,) = one - {common}
        slots[z, 0] = (a, common, b)
        slots[z, 1] = (b, common, a)
    return slots


def lookup(values, index):
    found = jnp.int32(int(values[0]))
    for i in range(1, len(values)):
        found = jnp.where(index == i, jnp.int32(int(values[i])), found)
    return found


def place():
    chip = lax.axis_index("tok").astype(jnp.int32)
    return lax.div(chip, N_X), lax.rem(chip, N_X), lax.axis_index("hid").astype(jnp.int32)


def block_at(plane, column, row):
    return lookup(slot_table().reshape(-1, 3)[:, row], plane * N_X + column)


def pack_kernel(far_routes, grads, inputs, p1_ref, p2_ref, p2_i_ref, x0_ref, own_ref, *scratch):
    routes_ref, held, held_i, packed, sems = scratch
    plane, column, core = place()
    capacity, total = x0_ref.shape
    width = held.shape[2]
    sources = [(grads, held, 0), (inputs, held_i, width)]
    copies = []
    for n, (source, buffer, _) in enumerate(sources):
        size = buffer.shape[2]
        for block in range(4):
            copies.append(
                pltpu.make_async_copy(
                    source.at[:, block * size : (block + 1) * size],
                    buffer.at[block],
                    sems.at[4 * n + block],
                )
            )
    routes_copy = pltpu.make_async_copy(far_routes, routes_ref, sems.at[8])
    routes_copy.start()
    for copy in copies:
        copy.start()
    routes_copy.wait()
    chosen = (routes_ref[0:1, :] == 0) | (routes_ref[1:2, :] == 0)
    tokens = chosen.shape[1]
    flags = jnp.where(chosen, 1.0, 0.0)
    before = (
        lax.broadcasted_iota(jnp.int32, (tokens, tokens), 0)
        <= lax.broadcasted_iota(jnp.int32, (tokens, tokens), 1)
    )
    rank = jnp.dot(
        flags.astype(BF16),
        jnp.where(before, 1.0, 0.0).astype(BF16),
        preferred_element_type=jnp.float32,
    )
    slot = lax.broadcasted_iota(jnp.int32, (capacity, tokens), 0).astype(jnp.float32) + 1.0
    picker = jnp.where((rank == slot) & chosen, 1.0, 0.0)
    empty = (jnp.sum(picker, axis=1, keepdims=True) == 0.0) & (
        lax.broadcasted_iota(jnp.int32, (capacity, 128), 1) == 0
    )
    picker = picker.astype(BF16)
    for n, (_, buffer, low) in enumerate(sources):
        for block in range(4):
            copies[4 * n + block].wait()
            got = jnp.dot(picker, buffer[block], preferred_element_type=jnp.float32)
            if n == 1:
                head = jnp.where(empty, jnp.inf, got[:, :128])
                packed[block, :, low : low + 128] = head.astype(BF16)
                packed[block, :, low + 128 :] = got[:, 128:].astype(BF16)
            else:
                packed[block, :, :width] = got.astype(BF16)
    to_plane = lax.rem(plane + jnp.where(core == 0, 1, 3), N_Z)
    for row in range(3):
        p1_ref[row] = packed[block_at(to_plane, column, row)]
    x0_block = jnp.where(
        core == 0, block_at(plane, 1 - column, 1), block_at(plane, 1 - column, 0)
    )
    x0_ref[...] = packed[x0_block]
    to_plane = lax.rem(plane + 2, N_Z)
    to_column = jnp.where(core == 0, column, 1 - column)
    for row in range(2):
        block = block_at(to_plane, to_column, row)
        p2_ref[row] = packed[block, :, :width]
        p2_i_ref[row] = packed[block, :, width:]
        own_ref[row] = packed[block_at(plane, column, row)]


BF16 = jnp.bfloat16


def pack(routes_t, grads, inputs, capacity):
    tokens = routes_t.shape[1]
    width, width_i = grads.shape[1] // 4, inputs.shape[1] // 4
    total = width + width_i
    shapes = [(3, capacity, total), (2, capacity, width), (2, capacity, width_i)]
    shapes += [(capacity, total), (2, capacity, total)]
    operands = [pltpu.with_memory_space_constraint(a, pltpu.HBM) for a in (routes_t, grads, inputs)]
    return pl.pallas_call(
        pack_kernel,
        out_shape=[jax.ShapeDtypeStruct(s, BF16) for s in shapes],
        in_specs=[pl.BlockSpec(memory_space=pltpu.HBM)] * 3,
        out_specs=[VMEM] * len(shapes),
        scratch_shapes=[
            pltpu.VMEM(routes_t.shape, jnp.int32),
            pltpu.VMEM((4, tokens, width), BF16),
            pltpu.VMEM((4, tokens, width_i), BF16),
            pltpu.VMEM((4, capacity, total), BF16),
            pltpu.SemaphoreType.DMA((9,)),
        ],
        compiler_params=pltpu.CompilerParams(vmem_limit_bytes=12 * 2**20),
        cost_estimate=pl.CostEstimate(
            flops=2 * 4 * capacity * tokens * total,
            bytes_accessed=8 * tokens * total,
            transcendentals=0,
        ),
    )(*operands)


def assemble(data, pieces, start):
    own, x0, hx0, p1, hp1, x1, hx1, p2, hp2 = pieces
    core = lax.axis_index("hid")
    capacity = own.shape[1]
    size = data.shape[2]
    span = pl.ds(start, size)
    for block in range(2):
        whole = [own.at[block], p1.at[block]]
        whole = [ref[:, span] for ref in whole]
        whole.append(jnp.where((core == 0) == (block == 1), x0[:, span], hx0[:, span]))
        whole += [hp1[block], x1[1 - block], hx1[1 - block], p2[block], hp2[block]]
        for slot, piece in enumerate(whole):
            low = slot * SLOT_ROWS
            data[block, low + 32 : low + SLOT_ROWS, :] = jnp.zeros((SLOT_ROWS - 32, size), BF16)
            data[block, low : low + capacity, :] = piece


def clear_marks(data, capacity, slots):
    for block in range(2):
        head = data[block, :, 0:128].astype(jnp.float32)
        gone = head == jnp.inf
        if block == 0:
            count = capacity * slots - jnp.sum(jnp.where(gone, 1.0, 0.0))
        data[block, :, 0:128] = jnp.where(gone, 0.0, head).astype(jnp.bfloat16)
    return 1.0 / count


def sides():
    plane, column, core = place()
    chip = plane * N_X + column
    first_ids, _ = block_table(4)
    first_is_common = lookup(
        (slot_table().reshape(-1, 3)[:, 0] != first_ids).astype(np.int32), chip
    )
    left = jnp.where(core == 0, first_is_common, 1 - first_is_common)
    return left, jnp.where(lax.rem(chip, 4) == 3, left, 1 - left)


def product(scale, left, right):
    return scale * lax.dot_general(
        left, right, (((0,), (0,)), ((), ())), preferred_element_type=jnp.float32
    )


def multiply(scale, data, out_ref, stage, sems, start):
    left, right = sides()
    steps = sems.shape[0]
    size = stage.shape[0] // steps
    copies = []
    for i in range(steps):
        rows = pl.ds(i * size, size)
        to = pl.ds(start + i * size, size)
        stage[rows, :] = product(scale, data[left, :, to], data[right])
        copies.append(pltpu.make_async_copy(stage.at[rows], out_ref.at[0, to], sems.at[i]))
        copies[-1].start()
    for copy in copies:
        copy.wait()


def cost(rows, width):
    return pl.CostEstimate(
        flops=2 * SLOTS * SLOT_ROWS * rows * width,
        bytes_accessed=4 * rows * width,
        transcendentals=0,
    )


def tile_kernel(marked, *refs):
    refs = list(refs)
    scale_in = None if marked else refs.pop(0)
    data, stage, sems = refs[-3:]
    pieces = refs[:9]
    out_ref = refs[9]
    assemble(data, pieces, pieces[0].shape[2] - data.shape[2] if marked else 0)
    if marked:
        scale = clear_marks(data, pieces[0].shape[1], SLOTS)
        refs[10][0] = scale
    else:
        scale = scale_in[0]
    multiply(scale, data, out_ref, stage, sems, 0)


def tile(scale, pieces, steps, limit):
    marked = scale is None
    width = pieces[-1].shape[2]
    out_shape = [jax.ShapeDtypeStruct((1, width, width), jnp.float32)]
    if marked:
        out_shape.append(jax.ShapeDtypeStruct((1,), jnp.float32))
    return pl.pallas_call(
        functools.partial(tile_kernel, marked),
        out_shape=out_shape,
        in_specs=([] if marked else [SMEM]) + [VMEM] * len(pieces),
        out_specs=[ANY, SMEM] if marked else [ANY],
        scratch_shapes=[
            pltpu.VMEM((2, SLOTS * SLOT_ROWS, width), BF16),
            pltpu.VMEM((width, width), jnp.float32),
            pltpu.SemaphoreType.DMA((steps,)),
        ],
        compiler_params=pltpu.CompilerParams(vmem_limit_bytes=limit),
        cost_estimate=cost(width, width),
    )(*([] if marked else [scale]), *pieces)


def moves(step):
    pairs = []
    for z in range(N_Z):
        for x in range(N_X):
            for core in range(2):
                to_z, to_x, to_core = step(z, x, core)
                source = (z * N_X + x) * 2 + core
                pairs.append((source, (to_z % N_Z * N_X + to_x) * 2 + to_core))
    return pairs


ALONG_Z = moves(lambda z, x, core: (z + (1, 3)[core], x, core))
ACROSS_Z = moves(lambda z, x, core: (z + 2, (x, 1 - x)[core], core))
ALONG_X = moves(lambda z, x, core: (z, 1 - x, core))
CORES = moves(lambda z, x, core: (z, x, 1 - core))


def after(array, *done):
    return lax.optimization_barrier((array, *done))[0]


def send(array, pairs):
    return lax.ppermute(array, ("tok", "hid"), pairs)


def both(array):
    return [array, send(array, CORES)]


def shards_eight(inputs, hidden_grads, routes):
    capacity = routes.shape[0] * 5 // 16
    width = hidden_grads.shape[1] // 4
    p1, p2, p2_i, x0, own = pack(routes.T, hidden_grads, inputs, capacity)
    p1 = send(p1, ALONG_Z)
    x0 = send(x0, ALONG_X)
    hx0 = send(x0, CORES)
    p1 = after(p1, x0)
    p2_i = send(after(p2_i, p1), ACROSS_Z)
    p2 = send(after(p2, p1), ACROSS_Z)
    x1_i = send(p1[1:, :, width:], ALONG_X)
    x1 = send(p1[1:, :, :width], ALONG_X)
    x1_i = after(x1_i, p2_i)
    hp1_i = send(p1[:2, :, width:], CORES)
    hp1 = send(p1[:2, :, :width], CORES)
    base = [own, x0, hx0, p1]
    input_tile, scale = tile(None, base + [hp1_i, *both(x1_i), *both(p2_i)], 3, 12 * 2**20)
    p2 = after(p2, scale)
    (grad_tile,) = tile(scale, base + [hp1, *both(x1), *both(p2)], 8, 28 * 2**20)
    return input_tile, grad_tile


def solution(mesh):
    placed = (P(("parts", "tok"), None), P(("parts", "tok"), None), P(("parts", "tok"), None))
    return jax.shard_map(
        shards_eight if mesh.shape["tok"] == N_X * N_Z else shards_any,
        mesh=mesh,
        in_specs=placed,
        out_specs=(P(("parts", "tok", "hid"), None, None), P(("parts", "tok", "hid"), None, None)),
        check_vma=False,
    )
```

```python
import functools
import math

import jax
import jax.numpy as jnp
import numpy as np
from jax import lax
from jax.experimental import pallas as pl
from jax.experimental.pallas import tpu as pltpu
from jax.sharding import PartitionSpec as P

SLOT_ROWS = 48


def block_table(side):
    first_list = []
    second_list = []
    for owner_chip in range(side * side // 2):
        stripe = owner_chip // side
        column = owner_chip % side
        if column == side - 1:
            first_list.append(stripe)
            second_list.append(side - 1 - stripe)
        elif column < side - 1 - stripe:
            first_list.append(stripe)
            second_list.append(stripe + 1 + column)
        else:
            first_list.append(side - 1 - stripe)
            second_list.append(column + 1)
    return (np.array(first_list, np.int32), np.array(second_list, np.int32))


def compact(values, chosen, capacity):
    ranking = jnp.cumsum(chosen) - 1
    slot_ids = jnp.arange(capacity, dtype=jnp.int32)
    picker = ((ranking[None, :] == slot_ids[:, None]) & (chosen[None, :] == 1)).astype(jnp.bfloat16)
    return jnp.dot(picker, values, preferred_element_type=jnp.float32).astype(jnp.bfloat16)


def outgoing(packed, side, first_ids, second_ids):
    slot_count, feature_count = packed.shape
    blocks = packed.reshape(slot_count, side, feature_count // side)
    return jnp.concatenate([blocks[:, first_ids], blocks[:, second_ids]], axis=2)


def block_product(flat_data, left_start, right_start, width):
    left = lax.dynamic_slice_in_dim(flat_data, left_start, width, 1)
    right = lax.dynamic_slice_in_dim(flat_data, right_start, width, 1)
    return lax.dot_general(
        left, right, (((0,), (0,)), ((), ())), preferred_element_type=jnp.float32
    )


def shards_any(inputs, hidden_grads, routes):
    chosen = jnp.any(routes == 0, axis=1).astype(jnp.int32)
    core_index = lax.axis_index("hid")
    chip_index = lax.axis_index("tok")
    device_count = lax.axis_size("tok")
    side = math.isqrt(2 * device_count)
    first_ids, second_ids = block_table(side)
    diagonal = chip_index % side == side - 1
    capacity = chosen.shape[0] * 5 // 16
    packed_inputs = compact(inputs, chosen, capacity)
    packed_grads = compact(hidden_grads, chosen, capacity)
    send_inputs = outgoing(packed_inputs, side, first_ids, second_ids)
    send_grads = outgoing(packed_grads, side, first_ids, second_ids)
    local_count = jnp.sum(chosen)
    got_inputs = lax.all_to_all(send_inputs, "tok", split_axis=1, concat_axis=1, tiled=True)
    total = lax.psum(local_count.astype(jnp.float32), "tok")
    got_grads = lax.all_to_all(send_grads, "tok", split_axis=1, concat_axis=1, tiled=True)
    flat_inputs = got_inputs.reshape(-1, got_inputs.shape[2])
    flat_grads = got_grads.reshape(-1, got_grads.shape[2])
    input_width = flat_inputs.shape[1] // 2
    grad_width = flat_grads.shape[1] // 2
    right_pick = jnp.where(diagonal, core_index, 1 - core_index)
    input_sum = block_product(
        flat_inputs, core_index * input_width, right_pick * input_width, input_width
    )
    grad_sum = block_product(flat_grads, core_index * grad_width, right_pick * grad_width, grad_width)
    return ((input_sum / total)[None], (grad_sum / total)[None])


N_X = 2
N_Z = 4
SLOTS = N_X * N_Z
SMEM = pl.BlockSpec(memory_space=pltpu.SMEM)
VMEM = pl.BlockSpec(memory_space=pltpu.VMEM)
ANY = pl.BlockSpec(memory_space=pl.ANY)


def slot_table():
    first_ids, second_ids = block_table(4)
    slots = np.zeros((N_Z, N_X, 3), np.int32)
    for z in range(N_Z):
        zero = {int(first_ids[z * N_X]), int(second_ids[z * N_X])}
        one = {int(first_ids[z * N_X + 1]), int(second_ids[z * N_X + 1])}
        common = max(zero & one)
        (a,) = zero - {common}
        (b,) = one - {common}
        slots[z, 0] = (a, common, b)
        slots[z, 1] = (b, common, a)
    return slots


FIRST_HOP = (2, 0, 3, 1)
SECOND_HOP = (1, 0, 3, 2)
ACROSS = (None, 2, 1, None)
OUTWARD = (None, 3, 0, None)


def first_slots():
    slots = slot_table()
    found = np.zeros((N_Z, N_X, 4), np.int32)
    found[:, :, :3] = slots
    for x in range(N_X):
        assert slots[1, x, 0] == slots[1, x, 2]
        found[1, x, 0] = slots[0, x, 0]
        found[1, x, 3] = slots[0, x, 2]
    return found.reshape(N_Z * N_X, 4)


def relay_slots():
    slots, first = slot_table(), first_slots().reshape(N_Z, N_X, 4)
    found = np.zeros((N_Z, N_X, 3), np.int32)
    for z in (1, 2):
        for x in range(N_X):
            held = [int(b) for b in first[z, x]]
            for row in range(3):
                found[z, x, row] = held.index(int(slots[SECOND_HOP[z], x, row]))
    return found.reshape(N_Z * N_X, 3)


def lookup(values, index):
    found = jnp.int32(int(values[0]))
    for i in range(1, len(values)):
        found = jnp.where(index == i, jnp.int32(int(values[i])), found)
    return found


def place():
    chip = lax.axis_index("tok").astype(jnp.int32)
    return lax.div(chip, N_X), lax.rem(chip, N_X), lax.axis_index("hid").astype(jnp.int32)


def block_at(plane, column, row):
    return lookup(slot_table().reshape(-1, 3)[:, row], plane * N_X + column)


def pack_kernel(far_routes, grads, inputs, *refs):
    first_ref, second_ref, across_ref, out_ref, x0_ref, own_ref = refs[:6]
    routes_ref, held, held_i, packed, sems = refs[6:]
    plane, column, core = place()
    capacity, total = x0_ref.shape
    width = held.shape[2]
    sources = [(grads, held), (inputs, held_i)]
    copies = []
    for n, (source, buffer) in enumerate(sources):
        size = buffer.shape[2]
        for block in range(4):
            copies.append(
                pltpu.make_async_copy(
                    source.at[:, block * size : (block + 1) * size],
                    buffer.at[block],
                    sems.at[4 * n + block],
                )
            )
    routes_copy = pltpu.make_async_copy(far_routes, routes_ref, sems.at[8])
    routes_copy.start()
    for copy in copies:
        copy.start()
    routes_copy.wait()
    chosen = (routes_ref[0:1, :] == 0) | (routes_ref[1:2, :] == 0)
    tokens = chosen.shape[1]
    flags = jnp.where(chosen, 1.0, 0.0)
    before = (
        lax.broadcasted_iota(jnp.int32, (tokens, tokens), 0)
        <= lax.broadcasted_iota(jnp.int32, (tokens, tokens), 1)
    )
    rank = jnp.dot(
        flags.astype(BF16),
        jnp.where(before, 1.0, 0.0).astype(BF16),
        preferred_element_type=jnp.float32,
    )
    slot = lax.broadcasted_iota(jnp.int32, (capacity, tokens), 0).astype(jnp.float32) + 1.0
    picker = jnp.where((rank == slot) & chosen, 1.0, 0.0)
    empty = (jnp.sum(picker, axis=1, keepdims=True) == 0.0) & (
        lax.broadcasted_iota(jnp.int32, (capacity, 128), 1) == 0
    )
    picker = picker.astype(BF16)
    for n, (_, buffer) in enumerate(sources):
        for block in range(4):
            copies[4 * n + block].wait()
            got = jnp.dot(picker, buffer[block], preferred_element_type=jnp.float32)
            if n == 0:
                head = jnp.where(empty, jnp.inf, got[:, :128])
                packed[block, :, :128] = head.astype(BF16)
                packed[block, :, 128:width] = got[:, 128:].astype(BF16)
            else:
                packed[block, :, width:] = got.astype(BF16)
    bounds = (0, width, total)

    def put_half(ref, row, block):
        for low, high in zip(bounds[:-1], bounds[1:]):
            half = (high - low) // 2
            start = pl.multiple_of(low + core * half, 128)
            ref[row, :, low // 2 : high // 2] = packed[block, :, pl.ds(start, half)]

    firsts = first_slots()
    to_plane = lookup(FIRST_HOP, plane)
    for row in range(4):
        put_half(first_ref, row, lookup(firsts[:, row], to_plane * N_X + column))
    to_plane = lookup(SECOND_HOP, plane)
    for row in range(3):
        put_half(second_ref, row, block_at(to_plane, column, row))
    x0_block = jnp.where(
        core == 0, block_at(plane, 1 - column, 1), block_at(plane, 1 - column, 0)
    )
    x0_ref[...] = packed[x0_block]
    to_column = jnp.where(core == 0, column, 1 - column)
    for row in range(2):
        own_ref[row] = packed[block_at(plane, column, row)]
        across_ref[row] = packed[block_at(lookup((0, 2, 1, 0), plane), to_column, row)]
        out_ref[row] = packed[block_at(lookup((0, 3, 0, 0), plane), to_column, row)]


BF16 = jnp.bfloat16


def pack(routes_t, grads, inputs, capacity):
    tokens = routes_t.shape[1]
    width, width_i = grads.shape[1] // 4, inputs.shape[1] // 4
    total = width + width_i
    shapes = [(4, capacity, total // 2), (3, capacity, total // 2), (2, capacity, total)]
    shapes += [(2, capacity, total), (capacity, total), (2, capacity, total)]
    operands = [pltpu.with_memory_space_constraint(a, pltpu.HBM) for a in (routes_t, grads, inputs)]
    return pl.pallas_call(
        pack_kernel,
        out_shape=[jax.ShapeDtypeStruct(s, BF16) for s in shapes],
        in_specs=[pl.BlockSpec(memory_space=pltpu.HBM)] * 3,
        out_specs=[VMEM] * len(shapes),
        scratch_shapes=[
            pltpu.VMEM(routes_t.shape, jnp.int32),
            pltpu.VMEM((4, tokens, width), BF16),
            pltpu.VMEM((4, tokens, width_i), BF16),
            pltpu.VMEM((4, capacity, total), BF16),
            pltpu.SemaphoreType.DMA((9,)),
        ],
        compiler_params=pltpu.CompilerParams(vmem_limit_bytes=12 * 2**20),
        cost_estimate=pl.CostEstimate(
            flops=2 * 4 * capacity * tokens * total,
            bytes_accessed=8 * tokens * total,
            transcendentals=0,
        ),
    )(*operands)


def relay_kernel(got, own, keep_ref, forward_ref, second_ref):
    plane, column, core = place()
    chip = plane * N_X + column
    table = relay_slots()
    inner = (plane == 1) | (plane == 2)
    keep_ref[0] = got[jnp.where(plane == 1, 2, 0)]
    keep_ref[1] = got[1]
    forward_ref[...] = got[1:3]
    for row in range(3):
        second_ref[row] = jnp.where(inner, got[lookup(table[:, row], chip)], own[row])


def relay(got, own):
    _, capacity, half = got.shape
    return pl.pallas_call(
        relay_kernel,
        out_shape=[jax.ShapeDtypeStruct((n, capacity, half), BF16) for n in (2, 2, 3)],
        in_specs=[VMEM] * 2,
        out_specs=[VMEM] * 3,
        compiler_params=pltpu.CompilerParams(vmem_limit_bytes=4 * 2**20),
        cost_estimate=cost(1, 1),
    )(got, own)


def assemble(data, pieces, start):
    own, x0, hx0, across, far_across, *halves, out, far_out = pieces
    plane, column, core = place()
    inner = (plane == 1) | (plane == 2)
    capacity = own.shape[1]
    size = data.shape[2]
    span = pl.ds(start, size)
    half = size // 2
    half_span = pl.ds(start // 2, half)
    mine = pl.ds(pl.multiple_of(core * half, 128), half)
    far = pl.ds(pl.multiple_of((1 - core) * half, 128), half)
    for block in range(2):
        whole = [own[block, :, span]]
        whole.append(jnp.where((core == 0) == (block == 1), x0[:, span], hx0[:, span]))
        whole.append(jnp.where(inner, across[block, :, span], out[block, :, span]))
        whole.append(jnp.where(inner, far_across[block, :, span], far_out[block, :, span]))
        for slot in range(SLOTS):
            low = slot * SLOT_ROWS
            data[block, low + 32 : low + SLOT_ROWS, :] = jnp.zeros((SLOT_ROWS - 32, size), BF16)
            if slot < len(whole):
                data[block, low : low + capacity, :] = whole[slot]
            else:
                n = 2 * (slot - len(whole))
                row = block if n < 4 else 1 - block
                rows = pl.ds(low, capacity)
                data[block, rows, mine] = halves[n][row, :, half_span]
                data[block, rows, far] = halves[n + 1][row, :, half_span]


def clear_marks(data, capacity, slots):
    for block in range(2):
        head = data[block, :, 0:128].astype(jnp.float32)
        gone = head == jnp.inf
        if block == 0:
            count = capacity * slots - jnp.sum(jnp.where(gone, 1.0, 0.0))
        data[block, :, 0:128] = jnp.where(gone, 0.0, head).astype(jnp.bfloat16)
    return 1.0 / count


def sides():
    plane, column, core = place()
    chip = plane * N_X + column
    first_ids, _ = block_table(4)
    first_is_common = lookup(
        (slot_table().reshape(-1, 3)[:, 0] != first_ids).astype(np.int32), chip
    )
    left = jnp.where(core == 0, first_is_common, 1 - first_is_common)
    return left, jnp.where(lax.rem(chip, 4) == 3, left, 1 - left)


def product(scale, left, right):
    return scale * lax.dot_general(
        left, right, (((0,), (0,)), ((), ())), preferred_element_type=jnp.float32
    )


def cost(rows, width):
    return pl.CostEstimate(flops=0, bytes_accessed=0, transcendentals=0)


def tiles_kernel(*refs):
    pieces = refs[:15]
    out_i, out, data, data_i, stage, stage_i, sems = refs[15:]
    left, right = sides()
    width = data.shape[2]
    copies = []

    def write(source, target):
        copies.append(pltpu.make_async_copy(source, target, sems.at[len(copies)]))
        copies[-1].start()

    def multiply(data, stage, out, steps):
        size = data.shape[2] // steps
        for i in range(steps):
            rows = pl.ds(i * size, size)
            stage[rows, :] = product(scale, data[left, :, rows], data[right])
            write(stage.at[rows], out.at[0, rows])

    assemble(data, pieces, 0)
    scale = clear_marks(data, pieces[0].shape[1], SLOTS)
    multiply(data, stage, out, 8)
    assemble(data_i, pieces, width)
    multiply(data_i, stage_i, out_i, 3)
    for copy in copies:
        copy.wait()


def tiles(width, pieces):
    width_i = pieces[0].shape[2] - width
    return pl.pallas_call(
        tiles_kernel,
        out_shape=[jax.ShapeDtypeStruct((1, w, w), jnp.float32) for w in (width_i, width)],
        in_specs=[VMEM] * len(pieces),
        out_specs=[ANY, ANY],
        scratch_shapes=[pltpu.VMEM((2, SLOTS * SLOT_ROWS, w), BF16) for w in (width, width_i)]
        + [pltpu.VMEM((w, w), jnp.float32) for w in (width, width_i)]
        + [pltpu.SemaphoreType.DMA((11,))],
        compiler_params=pltpu.CompilerParams(vmem_limit_bytes=32 * 2**20),
        cost_estimate=cost(width, width),
    )(*pieces)


def moves(step, turn=lambda x, core: (x, core)):
    pairs = []
    for z in range(N_Z):
        for x in range(N_X):
            for core in range(2):
                if step[z] is not None:
                    to_x, to_core = turn(x, core)
                    source = (z * N_X + x) * 2 + core
                    pairs.append((source, (step[z] * N_X + to_x) * 2 + to_core))
    return pairs


def to_both_columns(x, core):
    return (x, 1 - x)[core], core


def to_neighbour(x, core):
    return 1 - x, core


def to_other_core(x, core):
    return x, 1 - core


STAY = (0, 1, 2, 3)
FIRST = moves(FIRST_HOP)
SECOND = moves(SECOND_HOP)
MIDDLE = moves(ACROSS, to_both_columns)
ENDS = moves(OUTWARD, to_both_columns)
ALONG_X = moves(STAY, to_neighbour)
CORES = moves(STAY, to_other_core)
INNER_CORES = moves((None, 1, 2, None), to_other_core)
OUTER_CORES = moves((0, None, None, 3), to_other_core)


def after(array, *done):
    return lax.optimization_barrier((array, *done))[0]


def send(array, pairs):
    return lax.ppermute(array, ("tok", "hid"), pairs)


def shards_eight(inputs, hidden_grads, routes):
    capacity = routes.shape[0] * 5 // 16
    first, second, across, out, x0, own = pack(routes.T, hidden_grads, inputs, capacity)
    first = send(first, FIRST)
    x0 = send(x0, ALONG_X)
    hx0 = send(x0, CORES)
    first = after(first, x0)
    keep, forward, second = relay(first, second)
    second = send(second, SECOND)
    across = send(after(across, x0), MIDDLE)
    out = send(after(out, keep), ENDS)
    x1 = send(forward, ALONG_X)
    far_keep = send(keep, CORES)
    second = after(second, far_keep, hx0, across)
    far_x1 = send(x1, CORES)
    x2 = send(second[1:], ALONG_X)
    far_second = send(second[:2], CORES)
    far_across = send(across, INNER_CORES)
    far_x2 = send(x2, CORES)
    out = after(out, far_x1, far_second, far_across, far_x2)
    far_out = send(out, OUTER_CORES)
    pieces = [own, x0, hx0, across, far_across, keep, far_keep, second, far_second]
    pieces += [x1, far_x1, x2, far_x2, out, far_out]
    input_tile, grad_tile = tiles(hidden_grads.shape[1] // 4, pieces)
    return input_tile, grad_tile


def solution(mesh):
    placed = (P(("parts", "tok"), None), P(("parts", "tok"), None), P(("parts", "tok"), None))
    return jax.shard_map(
        shards_eight if mesh.shape["tok"] == N_X * N_Z else shards_any,
        mesh=mesh,
        in_specs=placed,
        out_specs=(P(("parts", "tok", "hid"), None, None), P(("parts", "tok", "hid"), None, None)),
        check_vma=False,
    )
```

```python
import functools
import math

import jax
import jax.numpy as jnp
import numpy as np
from jax import lax
from jax.experimental import pallas as pl
from jax.experimental.pallas import tpu as pltpu
from jax.sharding import PartitionSpec as P

SLOT_ROWS = 48


def block_table(side):
    first_list = []
    second_list = []
    for owner_chip in range(side * side // 2):
        stripe = owner_chip // side
        column = owner_chip % side
        if column == side - 1:
            first_list.append(stripe)
            second_list.append(side - 1 - stripe)
        elif column < side - 1 - stripe:
            first_list.append(stripe)
            second_list.append(stripe + 1 + column)
        else:
            first_list.append(side - 1 - stripe)
            second_list.append(column + 1)
    return (np.array(first_list, np.int32), np.array(second_list, np.int32))


def compact(values, chosen, capacity):
    ranking = jnp.cumsum(chosen) - 1
    slot_ids = jnp.arange(capacity, dtype=jnp.int32)
    picker = ((ranking[None, :] == slot_ids[:, None]) & (chosen[None, :] == 1)).astype(jnp.bfloat16)
    return jnp.dot(picker, values, preferred_element_type=jnp.float32).astype(jnp.bfloat16)


def outgoing(packed, side, first_ids, second_ids):
    slot_count, feature_count = packed.shape
    blocks = packed.reshape(slot_count, side, feature_count // side)
    return jnp.concatenate([blocks[:, first_ids], blocks[:, second_ids]], axis=2)


def block_product(flat_data, left_start, right_start, width):
    left = lax.dynamic_slice_in_dim(flat_data, left_start, width, 1)
    right = lax.dynamic_slice_in_dim(flat_data, right_start, width, 1)
    return lax.dot_general(
        left, right, (((0,), (0,)), ((), ())), preferred_element_type=jnp.float32
    )


def shards_any(inputs, hidden_grads, routes):
    chosen = jnp.any(routes == 0, axis=1).astype(jnp.int32)
    core_index = lax.axis_index("hid")
    chip_index = lax.axis_index("tok")
    device_count = lax.axis_size("tok")
    side = math.isqrt(2 * device_count)
    first_ids, second_ids = block_table(side)
    diagonal = chip_index % side == side - 1
    capacity = chosen.shape[0] * 5 // 16
    packed_inputs = compact(inputs, chosen, capacity)
    packed_grads = compact(hidden_grads, chosen, capacity)
    send_inputs = outgoing(packed_inputs, side, first_ids, second_ids)
    send_grads = outgoing(packed_grads, side, first_ids, second_ids)
    local_count = jnp.sum(chosen)
    got_inputs = lax.all_to_all(send_inputs, "tok", split_axis=1, concat_axis=1, tiled=True)
    total = lax.psum(local_count.astype(jnp.float32), "tok")
    got_grads = lax.all_to_all(send_grads, "tok", split_axis=1, concat_axis=1, tiled=True)
    flat_inputs = got_inputs.reshape(-1, got_inputs.shape[2])
    flat_grads = got_grads.reshape(-1, got_grads.shape[2])
    input_width = flat_inputs.shape[1] // 2
    grad_width = flat_grads.shape[1] // 2
    right_pick = jnp.where(diagonal, core_index, 1 - core_index)
    input_sum = block_product(
        flat_inputs, core_index * input_width, right_pick * input_width, input_width
    )
    grad_sum = block_product(flat_grads, core_index * grad_width, right_pick * grad_width, grad_width)
    return ((input_sum / total)[None], (grad_sum / total)[None])


N_X = 2
N_Z = 4
SLOTS = N_X * N_Z
IN_ROWS = (256,) * 3
GRAD_ROWS = (128,) * 2 + (256,) * 7
SMEM = pl.BlockSpec(memory_space=pltpu.SMEM)
VMEM = pl.BlockSpec(memory_space=pltpu.VMEM)
ANY = pl.BlockSpec(memory_space=pl.ANY)


def slot_table():
    first_ids, second_ids = block_table(4)
    slots = np.zeros((N_Z, N_X, 3), np.int32)
    for z in range(N_Z):
        zero = {int(first_ids[z * N_X]), int(second_ids[z * N_X])}
        one = {int(first_ids[z * N_X + 1]), int(second_ids[z * N_X + 1])}
        common = max(zero & one)
        (a,) = zero - {common}
        (b,) = one - {common}
        slots[z, 0] = (a, common, b)
        slots[z, 1] = (b, common, a)
    return slots


FIRST_HOP = (2, 0, 3, 1)
SECOND_HOP = (1, 0, 3, 2)
ACROSS = (None, 2, 1, None)
OUTWARD = (None, 3, 0, None)


def first_slots():
    slots = slot_table()
    found = np.zeros((N_Z, N_X, 4), np.int32)
    found[:, :, :3] = slots
    for x in range(N_X):
        assert slots[1, x, 0] == slots[1, x, 2]
        found[1, x, 0] = slots[0, x, 0]
        found[1, x, 3] = slots[0, x, 2]
    return found.reshape(N_Z * N_X, 4)


def relay_slots():
    slots, first = slot_table(), first_slots().reshape(N_Z, N_X, 4)
    found = np.zeros((N_Z, N_X, 3), np.int32)
    for z in (1, 2):
        for x in range(N_X):
            held = [int(b) for b in first[z, x]]
            for row in range(3):
                found[z, x, row] = held.index(int(slots[SECOND_HOP[z], x, row]))
    return found.reshape(N_Z * N_X, 3)


def lookup(values, index):
    found = jnp.int32(int(values[0]))
    for i in range(1, len(values)):
        found = jnp.where(index == i, jnp.int32(int(values[i])), found)
    return found


def place():
    chip = lax.axis_index("tok").astype(jnp.int32)
    return lax.div(chip, N_X), lax.rem(chip, N_X), lax.axis_index("hid").astype(jnp.int32)


BF16 = jnp.bfloat16
FAR = pl.BlockSpec(memory_space=pltpu.HBM)


def half_copies(sources, buffers, sems, which):
    copies = []
    for source, buffer in zip(sources, buffers):
        half = buffer.shape[2]
        for block in range(4):
            start = pl.multiple_of(block * 2 * half + which * half, 128)
            copies.append(
                pltpu.make_async_copy(
                    source.at[:, pl.ds(start, half)], buffer.at[block], sems.at[len(copies)]
                )
            )
    return copies


def choose(picker, empty, buffers, copies, packed, which):
    low = 0
    for n, buffer in enumerate(buffers):
        half = buffer.shape[2]
        for block in range(4):
            copies[4 * n + block].wait()
            got = jnp.dot(picker, buffer[block], preferred_element_type=jnp.float32)
            if n == 1:
                head = jnp.where(empty & (which == 0), jnp.inf, got[:, :128])
                packed[block, :, low : low + 128] = head.astype(BF16)
                packed[block, :, low + 128 :] = got[:, 128:].astype(BF16)
            else:
                packed[block, :, :half] = got.astype(BF16)
        low += half


def no_token(picker):
    capacity = picker.shape[0]
    return (jnp.sum(picker, axis=1, keepdims=True) == 0.0) & (
        lax.broadcasted_iota(jnp.int32, (capacity, 128), 1) == 0
    )


def pack_kernel(far_routes, grads, inputs, *refs):
    first_ref, second_ref, x0_ref, packed, picker_ref = refs[:5]
    routes_ref, held, held_i, sems = refs[5:]
    plane, column, core = place()
    capacity = packed.shape[1]
    routes_copy = pltpu.make_async_copy(far_routes, routes_ref, sems.at[8])
    routes_copy.start()
    copies = half_copies((grads, inputs), (held, held_i), sems, core)
    for copy in copies:
        copy.start()
    tokens = routes_ref.shape[1]
    before = (
        lax.broadcasted_iota(jnp.int32, (tokens, tokens), 0)
        <= lax.broadcasted_iota(jnp.int32, (tokens, tokens), 1)
    )
    before = jnp.where(before, 1.0, 0.0).astype(BF16)
    slot = lax.broadcasted_iota(jnp.int32, (capacity, tokens), 0).astype(jnp.float32) + 1.0
    routes_copy.wait()
    chosen = (routes_ref[0:1, :] == 0) | (routes_ref[1:2, :] == 0)
    flags = jnp.where(chosen, 1.0, 0.0)
    rank = jnp.dot(flags.astype(BF16), before, preferred_element_type=jnp.float32)
    picker = jnp.where((rank == slot) & chosen, 1.0, 0.0)
    empty = no_token(picker)
    picker = picker.astype(BF16)
    picker_ref[...] = picker
    choose(picker, empty, (held, held_i), copies, packed, core)
    firsts = first_slots()
    to_plane = lookup(FIRST_HOP, plane)
    for row in range(4):
        first_ref[row] = packed[lookup(firsts[:, row], to_plane * N_X + column)]
    to_plane = lookup(SECOND_HOP, plane)
    for row in range(3):
        second_ref[row] = packed[block_at(to_plane, column, row)]
    for row in range(2):
        x0_ref[row] = packed[block_at(plane, column, row + 1)]


def block_at(plane, column, row):
    return lookup(slot_table().reshape(-1, 3)[:, row], plane * N_X + column)


def pack(routes_t, grads, inputs, capacity):
    tokens = routes_t.shape[1]
    halves = (grads.shape[1] // 8, inputs.shape[1] // 8)
    shapes = [(n, capacity, sum(halves)) for n in (4, 3, 2, 4)] + [(capacity, tokens)]
    operands = [pltpu.with_memory_space_constraint(a, pltpu.HBM) for a in (routes_t, grads, inputs)]
    return pl.pallas_call(
        pack_kernel,
        out_shape=[jax.ShapeDtypeStruct(s, BF16) for s in shapes],
        in_specs=[FAR] * 3,
        out_specs=[VMEM] * len(shapes),
        scratch_shapes=[pltpu.VMEM(routes_t.shape, jnp.int32)]
        + [pltpu.VMEM((4, tokens, half), BF16) for half in halves]
        + [pltpu.SemaphoreType.DMA((9,))],
        compiler_params=pltpu.CompilerParams(vmem_limit_bytes=12 * 2**20),
        cost_estimate=NO_COST,
    )(*operands)


def rest_kernel(grads, inputs, packed, picker_ref, *refs):
    across_ref, out_ref, own_ref, held, held_i, other, whole, sems = refs
    plane, column, core = place()
    copies = half_copies((grads, inputs), (held, held_i), sems, 1 - core)
    for copy in copies:
        copy.start()
    halves = (held.shape[2], held_i.shape[2])
    spans = ((0, 0, halves[0]), (2 * halves[0], halves[0], halves[1]))
    picker = picker_ref[...]
    empty = no_token(picker.astype(jnp.float32))
    choose(picker, empty, (held, held_i), copies, other, 1 - core)
    for start, low, half in spans:
        mine = pl.ds(pl.multiple_of(start + core * half, 128), half)
        far = pl.ds(pl.multiple_of(start + (1 - core) * half, 128), half)
        for block in range(4):
            whole[block, :, mine] = packed[block, :, low : low + half]
            whole[block, :, far] = other[block, :, low : low + half]
    to_column = jnp.where(core == 0, column, 1 - column)
    for row in range(2):
        across_ref[row] = whole[block_at(lookup((0, 2, 1, 0), plane), to_column, row)]
        out_ref[row] = whole[block_at(lookup((0, 3, 0, 0), plane), to_column, row)]
        own_ref[row] = whole[block_at(plane, column, row)]


def rest(grads, inputs, packed, picker):
    _, capacity, half = packed.shape
    tokens = picker.shape[1]
    halves = (grads.shape[1] // 8, inputs.shape[1] // 8)
    shapes = [(2, capacity, 2 * half)] * 3
    operands = [pltpu.with_memory_space_constraint(a, pltpu.HBM) for a in (grads, inputs)]
    return pl.pallas_call(
        rest_kernel,
        out_shape=[jax.ShapeDtypeStruct(s, BF16) for s in shapes],
        in_specs=[FAR] * 2 + [VMEM] * 2,
        out_specs=[VMEM] * len(shapes),
        scratch_shapes=[pltpu.VMEM((4, tokens, h), BF16) for h in halves]
        + [pltpu.VMEM((4, capacity, half), BF16), pltpu.VMEM((4, capacity, 2 * half), BF16)]
        + [pltpu.SemaphoreType.DMA((8,))],
        compiler_params=pltpu.CompilerParams(vmem_limit_bytes=12 * 2**20),
        cost_estimate=NO_COST,
    )(*operands, packed, picker)


NO_COST = pl.CostEstimate(flops=0, bytes_accessed=0, transcendentals=0)


def relay_kernel(got, own, keep_ref, forward_ref, second_ref):
    plane, column, core = place()
    chip = plane * N_X + column
    table = relay_slots()
    inner = (plane == 1) | (plane == 2)
    keep_ref[0] = got[jnp.where(plane == 1, 2, 0)]
    keep_ref[1] = got[1]
    forward_ref[...] = got[1:3]
    for row in range(3):
        second_ref[row] = jnp.where(inner, got[lookup(table[:, row], chip)], own[row])


def relay(got, own):
    _, capacity, half = got.shape
    return pl.pallas_call(
        relay_kernel,
        out_shape=[jax.ShapeDtypeStruct((n, capacity, half), BF16) for n in (2, 2, 3)],
        in_specs=[VMEM] * 2,
        out_specs=[VMEM] * 3,
        compiler_params=pltpu.CompilerParams(vmem_limit_bytes=4 * 2**20),
        cost_estimate=NO_COST,
    )(got, own)


def assemble(data, pieces, start):
    own, across, far_across, out, far_out, *halves = pieces
    plane, column, core = place()
    inner = (plane == 1) | (plane == 2)
    capacity = own.shape[1]
    size = data.shape[2]
    span = pl.ds(start, size)
    half = size // 2
    half_span = pl.ds(start // 2, half)
    mine = pl.ds(pl.multiple_of(core * half, 128), half)
    far = pl.ds(pl.multiple_of((1 - core) * half, 128), half)

    def rows(slot):
        return pl.ds(slot * SLOT_ROWS, capacity)

    def put(slot, block, n):
        row = block if n % 2 else 1 - block
        data[block, rows(slot), mine] = halves[2 * n][row, :, half_span]
        data[block, rows(slot), far] = halves[2 * n + 1][row, :, half_span]

    for block in range(2):
        for slot in range(SLOTS):
            low = slot * SLOT_ROWS
            data[block, low + 32 : low + SLOT_ROWS, :] = jnp.zeros((SLOT_ROWS - 32, size), BF16)
        data[block, rows(0), :] = own[block, :, span]
        for n in range(5):
            put(1 + n, block, n)

    def put_whole(slot, ref):
        for block in range(2):
            data[block, rows(slot), :] = ref[block, :, span]

    @pl.when(inner)
    def _():
        put_whole(6, across)
        put_whole(7, far_across)

    @pl.when(jnp.logical_not(inner))
    def _():
        put_whole(6, out)
        put_whole(7, far_out)


def clear_marks(data, capacity, slots):
    for block in range(2):
        head = data[block, :, 0:128].astype(jnp.float32)
        gone = head == jnp.inf
        if block == 0:
            count = capacity * slots - jnp.sum(jnp.where(gone, 1.0, 0.0))
        data[block, :, 0:128] = jnp.where(gone, 0.0, head).astype(jnp.bfloat16)
    return 1.0 / count


def sides():
    plane, column, core = place()
    chip = plane * N_X + column
    first_ids, _ = block_table(4)
    first_is_common = lookup(
        (slot_table().reshape(-1, 3)[:, 0] != first_ids).astype(np.int32), chip
    )
    left = jnp.where(core == 0, first_is_common, 1 - first_is_common)
    return left, jnp.where(lax.rem(chip, 4) == 3, left, 1 - left)


def product(scale, left, right):
    return scale * lax.dot_general(
        left, right, (((0,), (0,)), ((), ())), preferred_element_type=jnp.float32
    )


def tiles_kernel(*refs):
    pieces = refs[:15]
    out_i, out, data, data_i, stage, stage_i, sems = refs[15:]
    left, right = sides()
    width = data.shape[2]
    copies = []

    def write(source, target):
        copies.append(pltpu.make_async_copy(source, target, sems.at[len(copies)]))
        copies[-1].start()

    def multiply(data, stage, out, sizes):
        low = 0
        for size in sizes:
            rows = pl.ds(low, size)
            low += size
            stage[rows, :] = product(scale, data[left, :, rows], data[right])
            write(stage.at[rows], out.at[0, rows])

    assemble(data_i, pieces, width)
    scale = clear_marks(data_i, pieces[0].shape[1], SLOTS)
    multiply(data_i, stage_i, out_i, IN_ROWS)
    assemble(data, pieces, 0)
    multiply(data, stage, out, GRAD_ROWS)
    for copy in copies:
        copy.wait()


def tiles(width, pieces):
    width_i = pieces[0].shape[2] - width
    return pl.pallas_call(
        tiles_kernel,
        out_shape=[jax.ShapeDtypeStruct((1, w, w), jnp.float32) for w in (width_i, width)],
        in_specs=[VMEM] * len(pieces),
        out_specs=[ANY, ANY],
        scratch_shapes=[pltpu.VMEM((2, SLOTS * SLOT_ROWS, w), BF16) for w in (width, width_i)]
        + [pltpu.VMEM((w, w), jnp.float32) for w in (width, width_i)]
        + [pltpu.SemaphoreType.DMA((len(IN_ROWS) + len(GRAD_ROWS),))],
        compiler_params=pltpu.CompilerParams(vmem_limit_bytes=32 * 2**20),
        cost_estimate=NO_COST,
    )(*pieces)


def moves(step, turn=lambda x, core: (x, core)):
    pairs = []
    for z in range(N_Z):
        for x in range(N_X):
            for core in range(2):
                if step[z] is not None:
                    to_x, to_core = turn(x, core)
                    source = (z * N_X + x) * 2 + core
                    pairs.append((source, (step[z] * N_X + to_x) * 2 + to_core))
    return pairs


def to_both_columns(x, core):
    return (x, 1 - x)[core], core


def to_neighbour(x, core):
    return 1 - x, core


def to_other_core(x, core):
    return x, 1 - core


STAY = (0, 1, 2, 3)
FIRST = moves(FIRST_HOP)
SECOND = moves(SECOND_HOP)
MIDDLE = moves(ACROSS, to_both_columns)
ENDS = moves(OUTWARD, to_both_columns)
ALONG_X = moves(STAY, to_neighbour)
CORES = moves(STAY, to_other_core)


def after(array, *done):
    return lax.optimization_barrier((array, *done))[0]


def send(array, pairs):
    return lax.ppermute(array, ("tok", "hid"), pairs)


def shards_eight(inputs, hidden_grads, routes):
    capacity = routes.shape[0] * 5 // 16
    first, second, x0, packed, picker = pack(routes.T, hidden_grads, inputs, capacity)
    first = send(first, FIRST)
    x0 = send(x0, ALONG_X)
    across, out, own = rest(hidden_grads, inputs, packed, picker)
    far_x0 = send(x0, CORES)
    first = after(first, x0)
    across = send(after(across, x0), MIDDLE)
    keep, forward, second = relay(first, second)
    second = send(second, SECOND)
    out = send(after(out, keep), ENDS)
    x1 = send(forward, ALONG_X)
    far_keep = send(keep, CORES)
    far_x1 = send(x1, CORES)
    second = after(second, far_keep, far_x0, across)
    x2 = send(second[1:], ALONG_X)
    far_second = send(second[:2], CORES)
    far_across = send(across, CORES)
    far_x2 = send(x2, CORES)
    out = after(out, far_x1, far_second, far_across, far_x2)
    far_out = send(out, CORES)
    pieces = [own, across, far_across, out, far_out, x0, far_x0, keep, far_keep]
    pieces += [x1, far_x1, second, far_second, x2, far_x2]
    return tuple(tiles(hidden_grads.shape[1] // 4, pieces))


def solution(mesh):
    placed = (P(("parts", "tok"), None), P(("parts", "tok"), None), P(("parts", "tok"), None))
    return jax.shard_map(
        shards_eight if mesh.shape["tok"] == N_X * N_Z else shards_any,
        mesh=mesh,
        in_specs=placed,
        out_specs=(P(("parts", "tok", "hid"), None, None), P(("parts", "tok", "hid"), None, None)),
        check_vma=False,
    )
```

```python
import functools
import math

import jax
import jax.numpy as jnp
import numpy as np
from jax import lax
from jax.experimental import pallas as pl
from jax.experimental.pallas import tpu as pltpu
from jax.sharding import PartitionSpec as P

SLOT_ROWS = 48


def block_table(side):
    first_list = []
    second_list = []
    for owner_chip in range(side * side // 2):
        stripe = owner_chip // side
        column = owner_chip % side
        if column == side - 1:
            first_list.append(stripe)
            second_list.append(side - 1 - stripe)
        elif column < side - 1 - stripe:
            first_list.append(stripe)
            second_list.append(stripe + 1 + column)
        else:
            first_list.append(side - 1 - stripe)
            second_list.append(column + 1)
    return (np.array(first_list, np.int32), np.array(second_list, np.int32))


def compact(values, chosen, capacity):
    ranking = jnp.cumsum(chosen) - 1
    slot_ids = jnp.arange(capacity, dtype=jnp.int32)
    picker = ((ranking[None, :] == slot_ids[:, None]) & (chosen[None, :] == 1)).astype(jnp.bfloat16)
    return jnp.dot(picker, values, preferred_element_type=jnp.float32).astype(jnp.bfloat16)


def outgoing(packed, side, first_ids, second_ids):
    slot_count, feature_count = packed.shape
    blocks = packed.reshape(slot_count, side, feature_count // side)
    return jnp.concatenate([blocks[:, first_ids], blocks[:, second_ids]], axis=2)


def block_product(flat_data, left_start, right_start, width):
    left = lax.dynamic_slice_in_dim(flat_data, left_start, width, 1)
    right = lax.dynamic_slice_in_dim(flat_data, right_start, width, 1)
    return lax.dot_general(
        left, right, (((0,), (0,)), ((), ())), preferred_element_type=jnp.float32
    )


def shards_any(inputs, hidden_grads, routes):
    chosen = jnp.any(routes == 0, axis=1).astype(jnp.int32)
    core_index = lax.axis_index("hid")
    chip_index = lax.axis_index("tok")
    device_count = lax.axis_size("tok")
    side = math.isqrt(2 * device_count)
    first_ids, second_ids = block_table(side)
    diagonal = chip_index % side == side - 1
    capacity = chosen.shape[0] * 5 // 16
    packed_inputs = compact(inputs, chosen, capacity)
    packed_grads = compact(hidden_grads, chosen, capacity)
    send_inputs = outgoing(packed_inputs, side, first_ids, second_ids)
    send_grads = outgoing(packed_grads, side, first_ids, second_ids)
    local_count = jnp.sum(chosen)
    got_inputs = lax.all_to_all(send_inputs, "tok", split_axis=1, concat_axis=1, tiled=True)
    total = lax.psum(local_count.astype(jnp.float32), "tok")
    got_grads = lax.all_to_all(send_grads, "tok", split_axis=1, concat_axis=1, tiled=True)
    flat_inputs = got_inputs.reshape(-1, got_inputs.shape[2])
    flat_grads = got_grads.reshape(-1, got_grads.shape[2])
    input_width = flat_inputs.shape[1] // 2
    grad_width = flat_grads.shape[1] // 2
    right_pick = jnp.where(diagonal, core_index, 1 - core_index)
    input_sum = block_product(
        flat_inputs, core_index * input_width, right_pick * input_width, input_width
    )
    grad_sum = block_product(flat_grads, core_index * grad_width, right_pick * grad_width, grad_width)
    return ((input_sum / total)[None], (grad_sum / total)[None])


N_X = 2
N_Z = 4
SLOTS = N_X * N_Z
IN_ROWS = (128,) * 6
GRAD_ROWS = (128,) * 4 + (256,) * 6
SMEM = pl.BlockSpec(memory_space=pltpu.SMEM)
VMEM = pl.BlockSpec(memory_space=pltpu.VMEM)
ANY = pl.BlockSpec(memory_space=pl.ANY)


def slot_table():
    first_ids, second_ids = block_table(4)
    slots = np.zeros((N_Z, N_X, 3), np.int32)
    for z in range(N_Z):
        zero = {int(first_ids[z * N_X]), int(second_ids[z * N_X])}
        one = {int(first_ids[z * N_X + 1]), int(second_ids[z * N_X + 1])}
        common = max(zero & one)
        (a,) = zero - {common}
        (b,) = one - {common}
        slots[z, 0] = (a, common, b)
        slots[z, 1] = (b, common, a)
    return slots


FIRST_HOP = (2, 0, 3, 1)
SECOND_HOP = (1, 0, 3, 2)
ACROSS = (None, 2, 1, None)
OUTWARD = (None, 3, 0, None)


def first_slots():
    slots = slot_table()
    found = np.zeros((N_Z, N_X, 4), np.int32)
    found[:, :, :3] = slots
    for x in range(N_X):
        assert slots[1, x, 0] == slots[1, x, 2]
        found[1, x, 0] = slots[0, x, 0]
        found[1, x, 3] = slots[0, x, 2]
    return found.reshape(N_Z * N_X, 4)


def relay_slots():
    slots, first = slot_table(), first_slots().reshape(N_Z, N_X, 4)
    found = np.zeros((N_Z, N_X, 3), np.int32)
    for z in (1, 2):
        for x in range(N_X):
            held = [int(b) for b in first[z, x]]
            for row in range(3):
                found[z, x, row] = held.index(int(slots[SECOND_HOP[z], x, row]))
    return found.reshape(N_Z * N_X, 3)


def lookup(values, index):
    found = jnp.int32(int(values[0]))
    for i in range(1, len(values)):
        found = jnp.where(index == i, jnp.int32(int(values[i])), found)
    return found


def place():
    chip = lax.axis_index("tok").astype(jnp.int32)
    return lax.div(chip, N_X), lax.rem(chip, N_X), lax.axis_index("hid").astype(jnp.int32)


BF16 = jnp.bfloat16
FAR = pl.BlockSpec(memory_space=pltpu.HBM)


def half_copies(sources, buffers, sems, which):
    copies = []
    for source, buffer in zip(sources, buffers):
        half = buffer.shape[2]
        for block in range(4):
            start = pl.multiple_of(block * 2 * half + which * half, 128)
            copies.append(
                pltpu.make_async_copy(
                    source.at[:, pl.ds(start, half)], buffer.at[block], sems.at[len(copies)]
                )
            )
    return copies


def choose(picker, empty, buffers, copies, packed, which):
    low = 0
    for n, buffer in enumerate(buffers):
        half = buffer.shape[2]
        for block in range(4):
            copies[4 * n + block].wait()
            got = jnp.dot(picker, buffer[block], preferred_element_type=jnp.float32)
            if n == 1:
                head = jnp.where(empty & (which == 0), jnp.inf, got[:, :128])
                packed[block, :, low : low + 128] = head.astype(BF16)
                packed[block, :, low + 128 :] = got[:, 128:].astype(BF16)
            else:
                packed[block, :, :half] = got.astype(BF16)
        low += half


def no_token(picker):
    capacity = picker.shape[0]
    return (jnp.sum(picker, axis=1, keepdims=True) == 0.0) & (
        lax.broadcasted_iota(jnp.int32, (capacity, 128), 1) == 0
    )


def pack_kernel(far_routes, grads, inputs, *refs):
    first_ref, second_ref, x0_ref, packed, picker_ref = refs[:5]
    routes_ref, held, held_i, sems = refs[5:]
    plane, column, core = place()
    capacity = packed.shape[1]
    routes_copy = pltpu.make_async_copy(far_routes, routes_ref, sems.at[8])
    routes_copy.start()
    copies = half_copies((grads, inputs), (held, held_i), sems, core)
    for copy in copies:
        copy.start()
    tokens = routes_ref.shape[1]
    before = (
        lax.broadcasted_iota(jnp.int32, (tokens, tokens), 0)
        <= lax.broadcasted_iota(jnp.int32, (tokens, tokens), 1)
    )
    before = jnp.where(before, 1.0, 0.0).astype(BF16)
    slot = lax.broadcasted_iota(jnp.int32, (capacity, tokens), 0).astype(jnp.float32) + 1.0
    routes_copy.wait()
    chosen = (routes_ref[0:1, :] == 0) | (routes_ref[1:2, :] == 0)
    flags = jnp.where(chosen, 1.0, 0.0)
    rank = jnp.dot(flags.astype(BF16), before, preferred_element_type=jnp.float32)
    picker = jnp.where((rank == slot) & chosen, 1.0, 0.0)
    empty = no_token(picker)
    picker = picker.astype(BF16)
    picker_ref[...] = picker
    choose(picker, empty, (held, held_i), copies, packed, core)
    firsts = first_slots()
    to_plane = lookup(FIRST_HOP, plane)
    for row in range(4):
        first_ref[row] = packed[lookup(firsts[:, row], to_plane * N_X + column)]
    to_plane = lookup(SECOND_HOP, plane)
    for row in range(3):
        second_ref[row] = packed[block_at(to_plane, column, row)]
    for row in range(2):
        x0_ref[row] = packed[block_at(plane, column, row + 1)]


def block_at(plane, column, row):
    return lookup(slot_table().reshape(-1, 3)[:, row], plane * N_X + column)


def pack(routes_t, grads, inputs, capacity):
    tokens = routes_t.shape[1]
    halves = (grads.shape[1] // 8, inputs.shape[1] // 8)
    shapes = [(n, capacity, sum(halves)) for n in (4, 3, 2, 4)] + [(capacity, tokens)]
    operands = [pltpu.with_memory_space_constraint(a, pltpu.HBM) for a in (routes_t, grads, inputs)]
    return pl.pallas_call(
        pack_kernel,
        out_shape=[jax.ShapeDtypeStruct(s, BF16) for s in shapes],
        in_specs=[FAR] * 3,
        out_specs=[VMEM] * len(shapes),
        scratch_shapes=[pltpu.VMEM(routes_t.shape, jnp.int32)]
        + [pltpu.VMEM((4, tokens, half), BF16) for half in halves]
        + [pltpu.SemaphoreType.DMA((9,))],
        compiler_params=pltpu.CompilerParams(vmem_limit_bytes=12 * 2**20),
        cost_estimate=NO_COST,
    )(*operands)


def rest_kernel(grads, inputs, packed, picker_ref, *refs):
    across_ref, out_ref, own_ref, held, held_i, other, whole, sems = refs
    plane, column, core = place()
    copies = half_copies((grads, inputs), (held, held_i), sems, 1 - core)
    for copy in copies:
        copy.start()
    halves = (held.shape[2], held_i.shape[2])
    spans = ((0, 0, halves[0]), (2 * halves[0], halves[0], halves[1]))
    picker = picker_ref[...]
    empty = no_token(picker.astype(jnp.float32))
    choose(picker, empty, (held, held_i), copies, other, 1 - core)
    for start, low, half in spans:
        mine = pl.ds(pl.multiple_of(start + core * half, 128), half)
        far = pl.ds(pl.multiple_of(start + (1 - core) * half, 128), half)
        for block in range(4):
            whole[block, :, mine] = packed[block, :, low : low + half]
            whole[block, :, far] = other[block, :, low : low + half]
    to_column = jnp.where(core == 0, column, 1 - column)
    for row in range(2):
        across_ref[row] = whole[block_at(lookup((0, 2, 1, 0), plane), to_column, row)]
        out_ref[row] = whole[block_at(lookup((0, 3, 0, 0), plane), to_column, row)]
        own_ref[row] = whole[block_at(plane, column, row)]


def rest(grads, inputs, packed, picker):
    _, capacity, half = packed.shape
    tokens = picker.shape[1]
    halves = (grads.shape[1] // 8, inputs.shape[1] // 8)
    shapes = [(2, capacity, 2 * half)] * 3
    operands = [pltpu.with_memory_space_constraint(a, pltpu.HBM) for a in (grads, inputs)]
    return pl.pallas_call(
        rest_kernel,
        out_shape=[jax.ShapeDtypeStruct(s, BF16) for s in shapes],
        in_specs=[FAR] * 2 + [VMEM] * 2,
        out_specs=[VMEM] * len(shapes),
        scratch_shapes=[pltpu.VMEM((4, tokens, h), BF16) for h in halves]
        + [pltpu.VMEM((4, capacity, half), BF16), pltpu.VMEM((4, capacity, 2 * half), BF16)]
        + [pltpu.SemaphoreType.DMA((8,))],
        compiler_params=pltpu.CompilerParams(vmem_limit_bytes=12 * 2**20),
        cost_estimate=NO_COST,
    )(*operands, packed, picker)


NO_COST = pl.CostEstimate(flops=0, bytes_accessed=0, transcendentals=0)


def relay_kernel(got, own, keep_ref, forward_ref, second_ref):
    plane, column, core = place()
    chip = plane * N_X + column
    table = relay_slots()
    inner = (plane == 1) | (plane == 2)
    keep_ref[0] = got[jnp.where(plane == 1, 2, 0)]
    keep_ref[1] = got[1]
    forward_ref[...] = got[1:3]
    for row in range(3):
        second_ref[row] = jnp.where(inner, got[lookup(table[:, row], chip)], own[row])


def relay(got, own):
    _, capacity, half = got.shape
    return pl.pallas_call(
        relay_kernel,
        out_shape=[jax.ShapeDtypeStruct((n, capacity, half), BF16) for n in (2, 2, 3)],
        in_specs=[VMEM] * 2,
        out_specs=[VMEM] * 3,
        compiler_params=pltpu.CompilerParams(vmem_limit_bytes=4 * 2**20),
        cost_estimate=NO_COST,
    )(got, own)


def assemble(data, pieces, start):
    own, across, far_across, out, far_out, *halves = pieces
    plane, column, core = place()
    inner = (plane == 1) | (plane == 2)
    capacity = own.shape[1]
    size = data.shape[2]
    span = pl.ds(start, size)
    half = size // 2
    half_span = pl.ds(start // 2, half)
    mine = pl.ds(pl.multiple_of(core * half, 128), half)
    far = pl.ds(pl.multiple_of((1 - core) * half, 128), half)

    def rows(slot):
        return pl.ds(slot * SLOT_ROWS, capacity)

    def put(slot, block, n):
        row = block if n % 2 else 1 - block
        data[block, rows(slot), mine] = halves[2 * n][row, :, half_span]
        data[block, rows(slot), far] = halves[2 * n + 1][row, :, half_span]

    for block in range(2):
        for slot in range(SLOTS):
            low = slot * SLOT_ROWS
            data[block, low + 32 : low + SLOT_ROWS, :] = jnp.zeros((SLOT_ROWS - 32, size), BF16)
        data[block, rows(0), :] = own[block, :, span]
        for n in range(5):
            put(1 + n, block, n)

    def put_whole(slot, ref):
        for block in range(2):
            data[block, rows(slot), :] = ref[block, :, span]

    @pl.when(inner)
    def _():
        put_whole(6, across)
        put_whole(7, far_across)

    @pl.when(jnp.logical_not(inner))
    def _():
        put_whole(6, out)
        put_whole(7, far_out)


def clear_marks(data, capacity, slots):
    for block in range(2):
        head = data[block, :, 0:128].astype(jnp.float32)
        gone = head == jnp.inf
        if block == 0:
            count = capacity * slots - jnp.sum(jnp.where(gone, 1.0, 0.0))
        data[block, :, 0:128] = jnp.where(gone, 0.0, head).astype(jnp.bfloat16)
    return 1.0 / count


def sides():
    plane, column, core = place()
    chip = plane * N_X + column
    first_ids, _ = block_table(4)
    first_is_common = lookup(
        (slot_table().reshape(-1, 3)[:, 0] != first_ids).astype(np.int32), chip
    )
    left = jnp.where(core == 0, first_is_common, 1 - first_is_common)
    return left, jnp.where(lax.rem(chip, 4) == 3, left, 1 - left)


def product(scale, left, right):
    return scale * lax.dot_general(
        left, right, (((0,), (0,)), ((), ())), preferred_element_type=jnp.float32
    )


def tiles_kernel(*refs):
    pieces = refs[:15]
    out_i, out, data, data_i, stage, stage_i, sems = refs[15:]
    left, right = sides()
    width = data.shape[2]
    copies = []

    def write(source, target):
        copies.append(pltpu.make_async_copy(source, target, sems.at[len(copies)]))
        copies[-1].start()

    def multiply(data, stage, out, sizes):
        low = 0
        for size in sizes:
            rows = pl.ds(low, size)
            low += size
            stage[rows, :] = product(scale, data[left, :, rows], data[right])
            write(stage.at[rows], out.at[0, rows])

    assemble(data_i, pieces, width)
    scale = clear_marks(data_i, pieces[0].shape[1], SLOTS)
    multiply(data_i, stage_i, out_i, IN_ROWS)
    assemble(data, pieces, 0)
    multiply(data, stage, out, GRAD_ROWS)
    for copy in copies:
        copy.wait()


def tiles(width, pieces):
    width_i = pieces[0].shape[2] - width
    return pl.pallas_call(
        tiles_kernel,
        out_shape=[jax.ShapeDtypeStruct((1, w, w), jnp.float32) for w in (width_i, width)],
        in_specs=[VMEM] * len(pieces),
        out_specs=[ANY, ANY],
        scratch_shapes=[pltpu.VMEM((2, SLOTS * SLOT_ROWS, w), BF16) for w in (width, width_i)]
        + [pltpu.VMEM((w, w), jnp.float32) for w in (width, width_i)]
        + [pltpu.SemaphoreType.DMA((len(IN_ROWS) + len(GRAD_ROWS),))],
        compiler_params=pltpu.CompilerParams(vmem_limit_bytes=32 * 2**20),
        cost_estimate=NO_COST,
    )(*pieces)


def moves(step, turn=lambda x, core: (x, core)):
    pairs = []
    for z in range(N_Z):
        for x in range(N_X):
            for core in range(2):
                if step[z] is not None:
                    to_x, to_core = turn(x, core)
                    source = (z * N_X + x) * 2 + core
                    pairs.append((source, (step[z] * N_X + to_x) * 2 + to_core))
    return pairs


def to_both_columns(x, core):
    return (x, 1 - x)[core], core


def to_neighbour(x, core):
    return 1 - x, core


def to_other_core(x, core):
    return x, 1 - core


STAY = (0, 1, 2, 3)
FIRST = moves(FIRST_HOP)
SECOND = moves(SECOND_HOP)
MIDDLE = moves(ACROSS, to_both_columns)
ENDS = moves(OUTWARD, to_both_columns)
ALONG_X = moves(STAY, to_neighbour)
CORES = moves(STAY, to_other_core)


def after(array, *done):
    return lax.optimization_barrier((array, *done))[0]


def send(array, pairs):
    return lax.ppermute(array, ("tok", "hid"), pairs)


def shards_eight(inputs, hidden_grads, routes):
    capacity = routes.shape[0] * 5 // 16
    first, second, x0, packed, picker = pack(routes.T, hidden_grads, inputs, capacity)
    first = send(first, FIRST)
    x0 = send(x0, ALONG_X)
    across, out, own = rest(hidden_grads, inputs, packed, picker)
    far_x0 = send(x0, CORES)
    first = after(first, x0)
    across = send(after(across, x0), MIDDLE)
    keep, forward, second = relay(first, second)
    second = send(second, SECOND)
    out = send(after(out, far_x0), ENDS)
    far_keep = send(keep, CORES)
    x1 = send(forward, ALONG_X)
    far_x1 = send(x1, CORES)
    second = after(second, far_keep, far_x0, across)
    x2 = send(second[1:], ALONG_X)
    far_second = send(second[:2], CORES)
    far_across = send(after(across, x2), CORES)
    far_x2 = send(x2, CORES)
    out = after(out, far_x1, far_second, far_x2)
    far_out = send(out, CORES)
    pieces = [own, across, far_across, out, far_out, x0, far_x0, keep, far_keep]
    pieces += [x1, far_x1, second, far_second, x2, far_x2]
    return tuple(tiles(hidden_grads.shape[1] // 4, pieces))


def solution(mesh):
    placed = (P(("parts", "tok"), None), P(("parts", "tok"), None), P(("parts", "tok"), None))
    return jax.shard_map(
        shards_eight if mesh.shape["tok"] == N_X * N_Z else shards_any,
        mesh=mesh,
        in_specs=placed,
        out_specs=(P(("parts", "tok", "hid"), None, None), P(("parts", "tok", "hid"), None, None)),
        check_vma=False,
    )
```

```python
import functools
import math

import jax
import jax.numpy as jnp
import numpy as np
from jax import lax
from jax.experimental import pallas as pl
from jax.experimental.pallas import tpu as pltpu
from jax.sharding import PartitionSpec as P

SLOT_ROWS = 48


def block_table(side):
    first_list = []
    second_list = []
    for owner_chip in range(side * side // 2):
        stripe = owner_chip // side
        column = owner_chip % side
        if column == side - 1:
            first_list.append(stripe)
            second_list.append(side - 1 - stripe)
        elif column < side - 1 - stripe:
            first_list.append(stripe)
            second_list.append(stripe + 1 + column)
        else:
            first_list.append(side - 1 - stripe)
            second_list.append(column + 1)
    return (np.array(first_list, np.int32), np.array(second_list, np.int32))


def compact(values, chosen, capacity):
    ranking = jnp.cumsum(chosen) - 1
    slot_ids = jnp.arange(capacity, dtype=jnp.int32)
    picker = ((ranking[None, :] == slot_ids[:, None]) & (chosen[None, :] == 1)).astype(jnp.bfloat16)
    return jnp.dot(picker, values, preferred_element_type=jnp.float32).astype(jnp.bfloat16)


def outgoing(packed, side, first_ids, second_ids):
    slot_count, feature_count = packed.shape
    blocks = packed.reshape(slot_count, side, feature_count // side)
    return jnp.concatenate([blocks[:, first_ids], blocks[:, second_ids]], axis=2)


def block_product(flat_data, left_start, right_start, width):
    left = lax.dynamic_slice_in_dim(flat_data, left_start, width, 1)
    right = lax.dynamic_slice_in_dim(flat_data, right_start, width, 1)
    return lax.dot_general(
        left, right, (((0,), (0,)), ((), ())), preferred_element_type=jnp.float32
    )


def shards_any(inputs, hidden_grads, routes):
    chosen = jnp.any(routes == 0, axis=1).astype(jnp.int32)
    core_index = lax.axis_index("hid")
    chip_index = lax.axis_index("tok")
    device_count = lax.axis_size("tok")
    side = math.isqrt(2 * device_count)
    first_ids, second_ids = block_table(side)
    diagonal = chip_index % side == side - 1
    capacity = chosen.shape[0] * 5 // 16
    packed_inputs = compact(inputs, chosen, capacity)
    packed_grads = compact(hidden_grads, chosen, capacity)
    send_inputs = outgoing(packed_inputs, side, first_ids, second_ids)
    send_grads = outgoing(packed_grads, side, first_ids, second_ids)
    local_count = jnp.sum(chosen)
    got_inputs = lax.all_to_all(send_inputs, "tok", split_axis=1, concat_axis=1, tiled=True)
    total = lax.psum(local_count.astype(jnp.float32), "tok")
    got_grads = lax.all_to_all(send_grads, "tok", split_axis=1, concat_axis=1, tiled=True)
    flat_inputs = got_inputs.reshape(-1, got_inputs.shape[2])
    flat_grads = got_grads.reshape(-1, got_grads.shape[2])
    input_width = flat_inputs.shape[1] // 2
    grad_width = flat_grads.shape[1] // 2
    right_pick = jnp.where(diagonal, core_index, 1 - core_index)
    input_sum = block_product(
        flat_inputs, core_index * input_width, right_pick * input_width, input_width
    )
    grad_sum = block_product(flat_grads, core_index * grad_width, right_pick * grad_width, grad_width)
    return ((input_sum / total)[None], (grad_sum / total)[None])


N_X = 2
N_Z = 4
SLOTS = N_X * N_Z
IN_ROWS = (128,) * 6
GRAD_ROWS = (128,) * 8 + (256,) * 4
SMEM = pl.BlockSpec(memory_space=pltpu.SMEM)
VMEM = pl.BlockSpec(memory_space=pltpu.VMEM)
ANY = pl.BlockSpec(memory_space=pl.ANY)


def slot_table():
    first_ids, second_ids = block_table(4)
    slots = np.zeros((N_Z, N_X, 3), np.int32)
    for z in range(N_Z):
        zero = {int(first_ids[z * N_X]), int(second_ids[z * N_X])}
        one = {int(first_ids[z * N_X + 1]), int(second_ids[z * N_X + 1])}
        common = max(zero & one)
        (a,) = zero - {common}
        (b,) = one - {common}
        slots[z, 0] = (a, common, b)
        slots[z, 1] = (b, common, a)
    return slots


FIRST_HOP = (2, 0, 3, 1)
SECOND_HOP = (1, 0, 3, 2)
ACROSS = (None, 2, 1, None)
OUTWARD = (None, 3, 0, None)


def first_slots():
    slots = slot_table()
    found = np.zeros((N_Z, N_X, 4), np.int32)
    found[:, :, :3] = slots
    for x in range(N_X):
        assert slots[1, x, 0] == slots[1, x, 2]
        found[1, x, 0] = slots[0, x, 0]
        found[1, x, 3] = slots[0, x, 2]
    return found.reshape(N_Z * N_X, 4)


def relay_slots():
    slots, first = slot_table(), first_slots().reshape(N_Z, N_X, 4)
    found = np.zeros((N_Z, N_X, 3), np.int32)
    for z in (1, 2):
        for x in range(N_X):
            held = [int(b) for b in first[z, x]]
            for row in range(3):
                found[z, x, row] = held.index(int(slots[SECOND_HOP[z], x, row]))
    return found.reshape(N_Z * N_X, 3)


def lookup(values, index):
    found = jnp.int32(int(values[0]))
    for i in range(1, len(values)):
        found = jnp.where(index == i, jnp.int32(int(values[i])), found)
    return found


def place():
    chip = lax.axis_index("tok").astype(jnp.int32)
    return lax.div(chip, N_X), lax.rem(chip, N_X), lax.axis_index("hid").astype(jnp.int32)


BF16 = jnp.bfloat16
FAR = pl.BlockSpec(memory_space=pltpu.HBM)


def half_copies(sources, buffers, sems, which):
    copies = []
    for source, buffer in zip(sources, buffers):
        half = buffer.shape[2]
        for block in range(4):
            start = pl.multiple_of(block * 2 * half + which * half, 128)
            copies.append(
                pltpu.make_async_copy(
                    source.at[:, pl.ds(start, half)], buffer.at[block], sems.at[len(copies)]
                )
            )
    return copies


def choose(picker, empty, buffers, copies, packed, which):
    low = 0
    for n, buffer in enumerate(buffers):
        half = buffer.shape[2]
        for block in range(4):
            copies[4 * n + block].wait()
            got = jnp.dot(picker, buffer[block], preferred_element_type=jnp.float32)
            if n == 1:
                head = jnp.where(empty & (which == 0), jnp.inf, got[:, :128])
                packed[block, :, low : low + 128] = head.astype(BF16)
                packed[block, :, low + 128 :] = got[:, 128:].astype(BF16)
            else:
                packed[block, :, :half] = got.astype(BF16)
        low += half


def no_token(picker):
    capacity = picker.shape[0]
    return (jnp.sum(picker, axis=1, keepdims=True) == 0.0) & (
        lax.broadcasted_iota(jnp.int32, (capacity, 128), 1) == 0
    )


def pack_kernel(far_routes, grads, inputs, *refs):
    first_ref, second_ref, x0_ref, packed, picker_ref = refs[:5]
    routes_ref, held, held_i, sems = refs[5:]
    plane, column, core = place()
    capacity = packed.shape[1]
    routes_copy = pltpu.make_async_copy(far_routes, routes_ref, sems.at[8])
    routes_copy.start()
    copies = half_copies((grads, inputs), (held, held_i), sems, core)
    for copy in copies:
        copy.start()
    tokens = routes_ref.shape[1]
    before = (
        lax.broadcasted_iota(jnp.int32, (tokens, tokens), 0)
        <= lax.broadcasted_iota(jnp.int32, (tokens, tokens), 1)
    )
    before = jnp.where(before, 1.0, 0.0).astype(BF16)
    slot = lax.broadcasted_iota(jnp.int32, (capacity, tokens), 0).astype(jnp.float32) + 1.0
    routes_copy.wait()
    chosen = (routes_ref[0:1, :] == 0) | (routes_ref[1:2, :] == 0)
    flags = jnp.where(chosen, 1.0, 0.0)
    rank = jnp.dot(flags.astype(BF16), before, preferred_element_type=jnp.float32)
    picker = jnp.where((rank == slot) & chosen, 1.0, 0.0)
    empty = no_token(picker)
    picker = picker.astype(BF16)
    picker_ref[...] = picker
    choose(picker, empty, (held, held_i), copies, packed, core)
    firsts = first_slots()
    to_plane = lookup(FIRST_HOP, plane)
    for row in range(4):
        first_ref[row] = packed[lookup(firsts[:, row], to_plane * N_X + column)]
    to_plane = lookup(SECOND_HOP, plane)
    for row in range(3):
        second_ref[row] = packed[block_at(to_plane, column, row)]
    for row in range(2):
        x0_ref[row] = packed[block_at(plane, column, row + 1)]


def block_at(plane, column, row):
    return lookup(slot_table().reshape(-1, 3)[:, row], plane * N_X + column)


def pack(routes_t, grads, inputs, capacity):
    tokens = routes_t.shape[1]
    halves = (grads.shape[1] // 8, inputs.shape[1] // 8)
    shapes = [(n, capacity, sum(halves)) for n in (4, 3, 2, 4)] + [(capacity, tokens)]
    operands = [pltpu.with_memory_space_constraint(a, pltpu.HBM) for a in (routes_t, grads, inputs)]
    return pl.pallas_call(
        pack_kernel,
        out_shape=[jax.ShapeDtypeStruct(s, BF16) for s in shapes],
        in_specs=[FAR] * 3,
        out_specs=[VMEM] * len(shapes),
        scratch_shapes=[pltpu.VMEM(routes_t.shape, jnp.int32)]
        + [pltpu.VMEM((4, tokens, half), BF16) for half in halves]
        + [pltpu.SemaphoreType.DMA((9,))],
        compiler_params=pltpu.CompilerParams(vmem_limit_bytes=12 * 2**20),
        cost_estimate=NO_COST,
    )(*operands)


def rest_kernel(grads, inputs, packed, picker_ref, *refs):
    across_ref, out_ref, own_ref, held, held_i, other, whole, sems = refs
    plane, column, core = place()
    copies = half_copies((grads, inputs), (held, held_i), sems, 1 - core)
    for copy in copies:
        copy.start()
    halves = (held.shape[2], held_i.shape[2])
    spans = ((0, 0, halves[0]), (2 * halves[0], halves[0], halves[1]))
    picker = picker_ref[...]
    empty = no_token(picker.astype(jnp.float32))
    choose(picker, empty, (held, held_i), copies, other, 1 - core)
    for start, low, half in spans:
        mine = pl.ds(pl.multiple_of(start + core * half, 128), half)
        far = pl.ds(pl.multiple_of(start + (1 - core) * half, 128), half)
        for block in range(4):
            whole[block, :, mine] = packed[block, :, low : low + half]
            whole[block, :, far] = other[block, :, low : low + half]
    to_column = jnp.where(core == 0, column, 1 - column)
    for row in range(2):
        across_ref[row] = whole[block_at(lookup((0, 2, 1, 0), plane), to_column, row)]
        out_ref[row] = whole[block_at(lookup((0, 3, 0, 0), plane), to_column, row)]
        own_ref[row] = whole[block_at(plane, column, row)]


def rest(grads, inputs, packed, picker):
    _, capacity, half = packed.shape
    tokens = picker.shape[1]
    halves = (grads.shape[1] // 8, inputs.shape[1] // 8)
    shapes = [(2, capacity, 2 * half)] * 3
    operands = [pltpu.with_memory_space_constraint(a, pltpu.HBM) for a in (grads, inputs)]
    return pl.pallas_call(
        rest_kernel,
        out_shape=[jax.ShapeDtypeStruct(s, BF16) for s in shapes],
        in_specs=[FAR] * 2 + [VMEM] * 2,
        out_specs=[VMEM] * len(shapes),
        scratch_shapes=[pltpu.VMEM((4, tokens, h), BF16) for h in halves]
        + [pltpu.VMEM((4, capacity, half), BF16), pltpu.VMEM((4, capacity, 2 * half), BF16)]
        + [pltpu.SemaphoreType.DMA((8,))],
        compiler_params=pltpu.CompilerParams(vmem_limit_bytes=12 * 2**20),
        cost_estimate=NO_COST,
    )(*operands, packed, picker)


NO_COST = pl.CostEstimate(flops=0, bytes_accessed=0, transcendentals=0)


def relay_kernel(got, own, keep_ref, forward_ref, second_ref):
    plane, column, core = place()
    chip = plane * N_X + column
    table = relay_slots()
    inner = (plane == 1) | (plane == 2)
    keep_ref[0] = got[jnp.where(plane == 1, 2, 0)]
    keep_ref[1] = got[1]
    forward_ref[...] = got[1:3]
    for row in range(3):
        second_ref[row] = jnp.where(inner, got[lookup(table[:, row], chip)], own[row])


def relay(got, own):
    _, capacity, half = got.shape
    return pl.pallas_call(
        relay_kernel,
        out_shape=[jax.ShapeDtypeStruct((n, capacity, half), BF16) for n in (2, 2, 3)],
        in_specs=[VMEM] * 2,
        out_specs=[VMEM] * 3,
        compiler_params=pltpu.CompilerParams(vmem_limit_bytes=4 * 2**20),
        cost_estimate=NO_COST,
    )(got, own)


def assemble(data, pieces, start):
    own, across, far_across, out, far_out, *halves = pieces
    plane, column, core = place()
    inner = (plane == 1) | (plane == 2)
    capacity = own.shape[1]
    size = data.shape[2]
    span = pl.ds(start, size)
    half = size // 2
    half_span = pl.ds(start // 2, half)
    mine = pl.ds(pl.multiple_of(core * half, 128), half)
    far = pl.ds(pl.multiple_of((1 - core) * half, 128), half)

    def rows(slot):
        return pl.ds(slot * SLOT_ROWS, capacity)

    def put(slot, block, n):
        row = block if n % 2 else 1 - block
        data[block, rows(slot), mine] = halves[2 * n][row, :, half_span]
        data[block, rows(slot), far] = halves[2 * n + 1][row, :, half_span]

    for block in range(2):
        for slot in range(SLOTS):
            low = slot * SLOT_ROWS
            data[block, low + 32 : low + SLOT_ROWS, :] = jnp.zeros((SLOT_ROWS - 32, size), BF16)
        data[block, rows(0), :] = own[block, :, span]
        for n in range(5):
            put(1 + n, block, n)

    def put_whole(slot, ref):
        for block in range(2):
            data[block, rows(slot), :] = ref[block, :, span]

    @pl.when(inner)
    def _():
        put_whole(6, across)
        put_whole(7, far_across)

    @pl.when(jnp.logical_not(inner))
    def _():
        put_whole(6, out)
        put_whole(7, far_out)


def clear_marks(data, capacity, slots):
    for block in range(2):
        head = data[block, :, 0:128].astype(jnp.float32)
        gone = head == jnp.inf
        if block == 0:
            count = capacity * slots - jnp.sum(jnp.where(gone, 1.0, 0.0))
        data[block, :, 0:128] = jnp.where(gone, 0.0, head).astype(jnp.bfloat16)
    return 1.0 / count


def sides():
    plane, column, core = place()
    chip = plane * N_X + column
    first_ids, _ = block_table(4)
    first_is_common = lookup(
        (slot_table().reshape(-1, 3)[:, 0] != first_ids).astype(np.int32), chip
    )
    left = jnp.where(core == 0, first_is_common, 1 - first_is_common)
    return left, jnp.where(lax.rem(chip, 4) == 3, left, 1 - left)


def product(scale, left, right):
    return scale * lax.dot_general(
        left, right, (((0,), (0,)), ((), ())), preferred_element_type=jnp.float32
    )


def tiles_kernel(*refs):
    pieces = refs[:15]
    out_i, out, data, data_i, stage, stage_i, sems = refs[15:]
    left, right = sides()
    width = data.shape[2]
    copies = []

    def write(source, target):
        copies.append(pltpu.make_async_copy(source, target, sems.at[len(copies)]))
        copies[-1].start()

    def multiply(data, stage, out, sizes):
        low = 0
        for size in sizes:
            rows = pl.ds(low, size)
            low += size
            stage[rows, :] = product(scale, data[left, :, rows], data[right])
            write(stage.at[rows], out.at[0, rows])

    assemble(data_i, pieces, width)
    scale = clear_marks(data_i, pieces[0].shape[1], SLOTS)
    multiply(data_i, stage_i, out_i, IN_ROWS)
    assemble(data, pieces, 0)
    multiply(data, stage, out, GRAD_ROWS)
    for copy in copies:
        copy.wait()


def tiles(width, pieces):
    width_i = pieces[0].shape[2] - width
    return pl.pallas_call(
        tiles_kernel,
        out_shape=[jax.ShapeDtypeStruct((1, w, w), jnp.float32) for w in (width_i, width)],
        in_specs=[VMEM] * len(pieces),
        out_specs=[ANY, ANY],
        scratch_shapes=[pltpu.VMEM((2, SLOTS * SLOT_ROWS, w), BF16) for w in (width, width_i)]
        + [pltpu.VMEM((w, w), jnp.float32) for w in (width, width_i)]
        + [pltpu.SemaphoreType.DMA((len(IN_ROWS) + len(GRAD_ROWS),))],
        compiler_params=pltpu.CompilerParams(vmem_limit_bytes=32 * 2**20),
        cost_estimate=NO_COST,
    )(*pieces)


def moves(step, turn=lambda x, core: (x, core)):
    pairs = []
    for z in range(N_Z):
        for x in range(N_X):
            for core in range(2):
                if step[z] is not None:
                    to_x, to_core = turn(x, core)
                    source = (z * N_X + x) * 2 + core
                    pairs.append((source, (step[z] * N_X + to_x) * 2 + to_core))
    return pairs


def to_both_columns(x, core):
    return (x, 1 - x)[core], core


def to_neighbour(x, core):
    return 1 - x, core


def to_other_core(x, core):
    return x, 1 - core


STAY = (0, 1, 2, 3)
FIRST = moves(FIRST_HOP)
SECOND = moves(SECOND_HOP)
MIDDLE = moves(ACROSS, to_both_columns)
ENDS = moves(OUTWARD, to_both_columns)
ALONG_X = moves(STAY, to_neighbour)
CORES = moves(STAY, to_other_core)


def after(array, *done):
    return lax.optimization_barrier((array, *done))[0]


def send(array, pairs):
    return lax.ppermute(array, ("tok", "hid"), pairs)


def shards_eight(inputs, hidden_grads, routes):
    capacity = routes.shape[0] * 5 // 16
    first, second, x0, packed, picker = pack(routes.T, hidden_grads, inputs, capacity)
    first = send(first, FIRST)
    x0 = send(x0, ALONG_X)
    across, out, own = rest(hidden_grads, inputs, packed, picker)
    far_x0 = send(x0, CORES)
    first = after(first, x0)
    across = send(after(across, x0), MIDDLE)
    keep, forward, second = relay(first, second)
    second = send(second, SECOND)
    out = send(after(out, far_x0), ENDS)
    far_keep = send(keep, CORES)
    x1 = send(forward, ALONG_X)
    far_x1 = send(x1, CORES)
    second = after(second, far_keep, far_x0, across)
    x2 = send(second[1:], ALONG_X)
    far_second = send(second[:2], CORES)
    far_across = send(after(across, x2), CORES)
    far_x2 = send(x2, CORES)
    out = after(out, far_x1, far_second, far_x2)
    far_out = send(out, CORES)
    pieces = [own, across, far_across, out, far_out, x0, far_x0, keep, far_keep]
    pieces += [x1, far_x1, second, far_second, x2, far_x2]
    return tuple(tiles(hidden_grads.shape[1] // 4, pieces))


def solution(mesh):
    placed = (P(("parts", "tok"), None), P(("parts", "tok"), None), P(("parts", "tok"), None))
    return jax.shard_map(
        shards_eight if mesh.shape["tok"] == N_X * N_Z else shards_any,
        mesh=mesh,
        in_specs=placed,
        out_specs=(P(("parts", "tok", "hid"), None, None), P(("parts", "tok", "hid"), None, None)),
        check_vma=False,
    )
```
